32 devices in a mesh: seq: 16 (over z, y, x), chan: 2 (over core).
Axes of the slice: x: 2, y: 2, z: 4, core: 2. Of those that a mesh axis runs over, the one named last changes fastest.
Arguments:
- query_proj: bfloat16 [2048, 2048], P('seq', 'chan'), may hold values from -70 to 70
- key_proj: bfloat16 [2048, 2048], P('seq', 'chan'), may hold values from -6 to 6
- value_proj: bfloat16 [2048, 2048], P('seq', 'chan'), may hold values from -6 to 6
- long_filter: float32 [2048, 2048], P('seq', 'chan'), may hold values from -0.125 to 0.125
- skip_gain: float32 [2048], P('chan'), may hold values from -1 to 1
- norm_gain: float32 [2048], P('chan'), may hold values from 0.25 to 1.75
- out_grad: bfloat16 [2048, 2048], P('seq', 'chan'), may hold values from -6 to 6
Outputs:
- block_out: bfloat16 [2048, 2048], P('seq', 'chan')
- query_grad: bfloat16 [2048, 2048], P('seq', 'chan')
- key_grad: bfloat16 [2048, 2048], P('seq', 'chan')
- value_grad: bfloat16 [2048, 2048], P('seq', 'chan')
- filter_grad: float32 [2048, 2048], P('seq', 'chan')
The draws below stay inside these ranges and needn't reach their ends.
All inputs are finite; a program needn't handle non-finite values.
Results may differ from the reference program's by a relative error of at most 0.0055.
Values sent between devices are 32-bit elements; how exact they have to be, the bound alone decides.
A program may use at most 128 MiB of HBM per device.

```python
import math
import jax
import jax.numpy as jnp
from jax import lax

SEQLEN = 2048
CHANNELS = 2048


def draw_query_proj(key, part):
    key = jax.random.fold_in(key, 11)
    scale_key, value_key = jax.random.split(key, 2)
    column_scale = jnp.exp(jax.random.uniform(scale_key, (1, CHANNELS), jnp.float32, 0.0, math.log(10.0)))
    base = jnp.clip(jax.random.normal(value_key, (SEQLEN, CHANNELS), jnp.float32), -6.0, 6.0)
    return (base * column_scale).astype(jnp.bfloat16)


def steps_of(stream_key, dims, pieces, smallest, top_value):
    factor_of = 1.0
    for dim, shards_of in pieces:
        steps = jax.random.uniform(jax.random.fold_in(jax.random.fold_in(stream_key, 6), dim), (shards_of,), jnp.float32, smallest / len(pieces), top_value / len(pieces))
        factor_of = factor_of * jnp.repeat(jnp.exp(steps), dims[dim] // shards_of).reshape((-1,) + (1,) * (len(dims) - 1 - dim))
    return factor_of


def normal_values(key, dims, deviation, bound, shards=(), dtype=jnp.bfloat16):
    loudness = steps_of(key, dims, shards, -0.22, 0.18) if shards else 1.0
    drawn = jax.random.normal(key, dims, jnp.float32) * deviation * loudness
    return jnp.minimum(jnp.maximum(drawn, -bound), bound).astype(dtype)


def setup_inputs(seed: int = 0) -> dict:
    streams_of = jax.random.split(jax.random.key(seed), 8)
    query_proj = draw_query_proj(jax.random.fold_in(streams_of[7], 71), 0)
    key_proj = normal_values(streams_of[1], (SEQLEN, CHANNELS), 1.0, 6.0, ((0, 16), (1, 2)))
    value_proj = normal_values(streams_of[2], (SEQLEN, CHANNELS), 1.0, 6.0, ((0, 16), (1, 2)))
    long_filter = normal_values(streams_of[3], (SEQLEN, CHANNELS), SEQLEN ** -0.5, 0.125, ((0, 16), (1, 2)), jnp.float32)
    skip_gain = jnp.clip(jax.random.uniform(streams_of[4], (CHANNELS,), jnp.float32, -1.0, 1.0) * steps_of(streams_of[4], (CHANNELS,), ((0, 2),), -0.4, 0.0), -1.0, 1.0)
    norm_gain = jnp.clip(1.0 + 0.15 * jax.random.normal(streams_of[5], (CHANNELS,), jnp.float32), 0.25, 1.75)
    out_grad = normal_values(streams_of[6], (SEQLEN, CHANNELS), 1.0, 6.0, ((0, 16), (1, 2)))
    return {"query_proj": query_proj, "key_proj": key_proj, "value_proj": value_proj, "long_filter": long_filter, "skip_gain": skip_gain, "norm_gain": norm_gain, "out_grad": out_grad}


def reference(query_proj, key_proj, value_proj, long_filter, skip_gain, norm_gain, out_grad):
    length = SEQLEN
    queries = query_proj.astype(jnp.float32)
    key_rows = key_proj.astype(jnp.float32)
    values = value_proj.astype(jnp.float32)
    gated_in = key_rows * values

    def spectrum(signal):
        return jnp.fft.rfft(signal, n=2 * length, axis=0)

    def back_to_rows(spec):
        return jnp.fft.irfft(spec, n=2 * length, axis=0)[:length]
    gated_spec = spectrum(gated_in)
    filter_spec = spectrum(long_filter)
    convolved = back_to_rows(gated_spec * filter_spec)
    mixed = convolved + skip_gain[None, :] * gated_in
    activated = queries * mixed
    inverse_rms = lax.rsqrt(lax.optimization_barrier(jnp.mean(activated * activated, axis=1, keepdims=True)) + 1e-05)
    block_out = (activated * inverse_rms * norm_gain[None, :]).astype(jnp.bfloat16)
    scaled_grad = out_grad.astype(jnp.float32) * norm_gain[None, :]
    cross_mean = lax.optimization_barrier(jnp.mean(scaled_grad * activated, axis=1, keepdims=True))
    act_grad = inverse_rms * scaled_grad - activated * inverse_rms ** 3 * cross_mean
    query_grad = (act_grad * mixed).astype(jnp.bfloat16)
    mix_grad = act_grad * queries
    grad_spec = spectrum(mix_grad)
    input_part = back_to_rows(grad_spec * jnp.conj(filter_spec))
    filter_grad = back_to_rows(grad_spec * jnp.conj(gated_spec))
    gated_grad = input_part + skip_gain[None, :] * mix_grad
    key_grad = (gated_grad * values).astype(jnp.bfloat16)
    value_grad = (gated_grad * key_rows).astype(jnp.bfloat16)
    return (block_out, query_grad, key_grad, value_grad, filter_grad)
```

```python
import functools
import math

import jax
import jax.numpy as jnp
import numpy as np
from jax import lax
from jax.experimental import pallas as pl
from jax.experimental.pallas import tpu as pltpu
from jax.sharding import PartitionSpec as P

exact_mode = lax.Precision.HIGHEST
epsilon_value = 1e-05


def dft_matrix(count, sign):
    indices = jnp.arange(count, dtype=jnp.int32)
    product = indices[:, None] * indices[None, :] % count
    angles = product.astype(jnp.float32) * (2.0 * math.pi / count)
    cosine = jnp.cos(angles)
    sine_part = sign * jnp.sin(angles)
    return jnp.stack([jnp.stack([cosine, -sine_part], 1), jnp.stack([sine_part, cosine], 1)], 0)


def rotate(field, angles):
    cos_part = jnp.cos(angles)
    sin_part = jnp.sin(angles)
    real_part = field[:, 0]
    imag_part = field[:, 1]
    return jnp.stack(
        [real_part * cos_part - imag_part * sin_part, real_part * sin_part + imag_part * cos_part],
        1,
    )


def prepare(signals, positions, length):
    angles = (positions.astype(jnp.float32) * (-math.pi / length))[..., None]
    cos_part = jnp.cos(angles)
    sin_part = jnp.sin(angles)
    real_in = signals[:, 0]
    real_part = jnp.stack([real_in, real_in * cos_part], 1)
    imag_part = jnp.stack([jnp.zeros_like(real_in), real_in * sin_part], 1)
    return jnp.stack([real_part, imag_part], 1)


def finish(field, positions, length):
    angles = (positions.astype(jnp.float32) * (math.pi / length))[..., None]
    second = rotate(field[:, :, 1], angles)
    return (field[:, :, 0] + second) / (2.0 * length)


def complex_product(first, second, conjugate):
    second_imag = -second[1] if conjugate else second[1]
    return jnp.stack(
        [
            first[0] * second[0] - first[1] * second_imag,
            first[0] * second_imag + first[1] * second[0],
        ],
        0,
    )


def wide_body(query_proj, key_proj, value_proj, long_filter, skip_gain, norm_gain, out_grad):
    tok_rows, chan_width = query_proj.shape
    seq_count = lax.axis_size("seq")
    seq_index = lax.axis_index("seq")
    length = tok_rows * seq_count
    channel_total = chan_width * lax.axis_size("chan")
    narrow_rows = tok_rows // seq_count
    forward_rows = dft_matrix(tok_rows, -1.0)
    inverse_rows = dft_matrix(tok_rows, 1.0)

    def block_places():
        offsets = seq_index * narrow_rows + jnp.arange(narrow_rows, dtype=jnp.int32)
        return jnp.arange(seq_count, dtype=jnp.int32)[:, None] * tok_rows + offsets[None, :]

    def channel_forward(signals):
        batch, width = (signals.shape[0], signals.shape[1])
        blocks = signals.reshape(batch, width, seq_count, narrow_rows, chan_width)
        spread = lax.all_to_all(blocks, "seq", split_axis=2, concat_axis=2, tiled=True)
        field = prepare(spread, block_places(), length)
        field = jnp.einsum(
            "pkqn,bqsnjc->bpskjc", dft_matrix(seq_count, -1.0), field, precision=exact_mode
        )
        offsets = seq_index * narrow_rows + jnp.arange(narrow_rows, dtype=jnp.int32)
        turns = jnp.arange(seq_count, dtype=jnp.int32)[:, None] * offsets[None, :] % length
        field = rotate(field, (turns.astype(jnp.float32) * (-2.0 * math.pi / length))[:, :, None])
        field = lax.all_to_all(field, "seq", split_axis=3, concat_axis=3, tiled=True)
        field = field.reshape(batch, 2, 2, tok_rows, chan_width)
        return jnp.einsum("pkqr,bqsrc->bpskc", forward_rows, field, precision=exact_mode)

    def channel_inverse(spectra, parts):
        batch = spectra.shape[0]
        field = jnp.einsum("pkqr,bqsrc->bpskc", inverse_rows, spectra, precision=exact_mode)
        turns = seq_index * jnp.arange(tok_rows, dtype=jnp.int32) % length
        field = rotate(field, (turns.astype(jnp.float32) * (2.0 * math.pi / length))[:, None])
        field = field.reshape(batch, 2, 2, seq_count, narrow_rows, chan_width)
        field = lax.all_to_all(field, "seq", split_axis=3, concat_axis=3, tiled=True)
        field = jnp.einsum(
            "pkqn,bqsnjc->bpskjc", dft_matrix(seq_count, 1.0), field, precision=exact_mode
        )
        result = finish(field, block_places(), length)[:, :parts]
        result = lax.all_to_all(result, "seq", split_axis=2, concat_axis=2, tiled=True)
        return result.reshape(batch, parts, tok_rows, chan_width)

    def transform(signals):
        return channel_forward(signals)

    def untransform(spectra, parts):
        return channel_inverse(spectra, parts)

    queries = query_proj.astype(jnp.float32)
    key_rows = key_proj.astype(jnp.float32)
    values = value_proj.astype(jnp.float32)
    gated_in = key_rows * values
    spectra = transform(jnp.stack([gated_in, long_filter], 0)[:, None])
    gated_spec = spectra[0]
    filter_spec = spectra[1]
    mixed_spec = complex_product(gated_spec, filter_spec, False)
    convolved = untransform(mixed_spec[None], 1)[0, 0]
    mixed = convolved + skip_gain[None, :] * gated_in
    activated = queries * mixed
    squares = lax.psum(jnp.sum(activated * activated, axis=1), "chan")
    inverse_rms = lax.rsqrt(squares / channel_total + epsilon_value)[:, None]
    block_out = (activated * inverse_rms * norm_gain[None, :]).astype(jnp.bfloat16)
    scaled_grad = out_grad.astype(jnp.float32) * norm_gain[None, :]
    cross_sum = lax.psum(jnp.sum(scaled_grad * activated, axis=1), "chan")
    cross_mean = (cross_sum / channel_total)[:, None]
    act_grad = inverse_rms * scaled_grad - activated * inverse_rms**3 * cross_mean
    query_grad = (act_grad * mixed).astype(jnp.bfloat16)
    mix_grad = act_grad * queries
    grad_spec = transform(mix_grad[None, None])[0]
    toward_input = complex_product(grad_spec, filter_spec, True)
    toward_filter = complex_product(grad_spec, gated_spec, True)
    results = untransform(jnp.stack([toward_input, toward_filter], 0), 1)
    input_part = results[0, 0]
    filter_grad = results[1, 0]
    gated_grad = input_part + skip_gain[None, :] * mix_grad
    key_grad = (gated_grad * values).astype(jnp.bfloat16)
    value_grad = (gated_grad * key_rows).astype(jnp.bfloat16)
    return (block_out, query_grad, key_grad, value_grad, filter_grad)


MESH = pl.DeviceIdType.MESH
GATED, FILTER, CONV, MIXGRAD, INPUT, FGRAD = range(6)


def split_matrix(matrix):
    matrix = jnp.asarray(matrix, jnp.float32)
    high = matrix.astype(jnp.bfloat16)
    low = (matrix - high.astype(jnp.float32)).astype(jnp.bfloat16)
    return jnp.concatenate([high, low, high], 1)


def block_matrices(rows):
    freqs = 2 * np.arange(rows) + 1
    places = np.arange(2 * rows)
    angles = np.pi / (2 * rows) * (freqs[:, None] * places[None, :] % (4 * rows))
    forward = np.concatenate([np.cos(angles), -np.sin(angles)], 0)[:, :rows]
    inverse = np.concatenate([np.cos(angles), -np.sin(angles)], 0).T / rows
    return split_matrix(forward), split_matrix(inverse)


def split_dot(matrix, values):
    high = values.astype(jnp.bfloat16)
    low = (values - high.astype(jnp.float32)).astype(jnp.bfloat16)
    return jnp.dot(
        matrix, jnp.concatenate([high, high, low], 0), preferred_element_type=jnp.float32
    )


def fast_kernel(
    seq_count,
    q_ref, k_ref, v_ref, f_ref, skip_ref, norm_ref, g_ref, fwd_ref, inv_ref,
    out_ref, qg_ref, kg_ref, vg_ref, fg_ref,
    send, recv, h_spec, h_swap, x_spec, x_swap, m_spec, m_swap, z_spec, fields,
    mixed_ref, mix_ref, stat_send, stat_recv,
    send_sems, recv_sems, stat_sems,
):
    rows, width = q_ref.shape
    half = rows // 2
    pairs = seq_count // 2
    channel_total = 2 * width
    me = lax.axis_index("seq")
    core = lax.axis_index("chan")
    f32 = jnp.float32

    barrier = pltpu.get_barrier_semaphore()

    def greet(step, carry):
        peer = lax.rem(me + step, seq_count)
        pl.semaphore_signal(barrier, inc=1, device_id={"seq": peer}, device_id_type=MESH)
        return carry

    lax.fori_loop(1, seq_count, greet, 0)
    pl.semaphore_signal(barrier, inc=1, device_id={"chan": 1 - core}, device_id_type=MESH)

    def first_lanes(count):
        return lax.broadcasted_iota(jnp.int32, (count, 128), 1) < 64

    def swap(values):
        return pltpu.roll(values, 64, 1)

    def lanes(tile):
        return pl.ds(pl.multiple_of(tile * 128, 128), 128)

    def pack(unit, tile, values):
        top, bottom = values[:half], values[half:]
        left = first_lanes(half)
        send[unit, 2 * tile] = jnp.where(left, top, swap(bottom))
        send[unit, 2 * tile + 1] = jnp.where(left, swap(top), bottom)

    def unpack(unit, tile):
        first, second = recv[unit, 2 * tile], recv[unit, 2 * tile + 1]
        left = first_lanes(half)
        return jnp.concatenate(
            [jnp.where(left, first, swap(second)), jnp.where(left, swap(first), second)], 0
        )

    def remote(unit, src, dst, peer, send_slot, recv_slot):
        return pltpu.make_async_remote_copy(
            src_ref=send.at[unit, src],
            dst_ref=recv.at[unit, dst],
            send_sem=send_sems.at[unit, send_slot],
            recv_sem=recv_sems.at[unit, recv_slot],
            device_id={"seq": peer},
            device_id_type=MESH,
        )

    def send_all(unit):
        def one(step, carry):
            peer = lax.rem(me + step, seq_count)
            remote(unit, peer, me, peer, peer, me).start()
            return carry

        lax.fori_loop(1, seq_count, one, 0)
        recv[unit, me] = send[unit, me]

    def receive_all(unit):
        def one(step, carry):
            peer = lax.rem(me + seq_count - step, seq_count)
            remote(unit, peer, peer, peer, peer, peer).wait_recv()
            return carry

        lax.fori_loop(1, seq_count, one, 0)

    def sent_all(unit):
        def one(step, carry):
            peer = lax.rem(me + step, seq_count)
            remote(unit, peer, me, peer, peer, me).wait_send()
            return carry

        lax.fori_loop(1, seq_count, one, 0)

    def spectrum(unit, spec, swapped):
        def one(step, carry):
            block = jnp.concatenate([unpack(unit, 2 * step), unpack(unit, 2 * step + 1)], 1)
            field = split_dot(fwd_ref[...], block)
            for side in range(2):
                part = field[:, 128 * side:128 * side + 128]
                spec[2 * step + side] = part
                swapped[2 * step + side] = swap(part)
            return carry

        lax.fori_loop(0, pairs // 2, one, 0)

    def load(ref, tile, count):
        first = pl.multiple_of(tile * 8, 8)
        real = [ref[k, pl.ds(first, 8), :] for k in range(count)]
        imag = [ref[k, pl.ds(first + rows, 8), :] for k in range(count)]
        return real, imag

    def convolve():
        def one(tile, carry):
            left = first_lanes(8)
            zero = jnp.zeros((8, 128), f32)
            hr, hi = load(h_spec, tile, pairs)
            sr, si = load(h_swap, tile, pairs)
            xr, xi = load(x_spec, tile, pairs)
            yr, yi = load(x_swap, tile, pairs)
            even = [
                (jnp.where(left, hr[k], sr[k]), jnp.where(left, hi[k], si[k]))
                for k in range(pairs)
            ]
            odd = [
                (
                    jnp.where(left, sr[k - 1] if k else zero, hr[k]),
                    jnp.where(left, si[k - 1] if k else zero, hi[k]),
                )
                for k in range(pairs)
            ]
            first = pl.multiple_of(tile * 8, 8)
            for n in range(pairs):
                real, imag = zero, zero
                for k in range(n + 1):
                    er, ei = even[k]
                    tr, ti = odd[k]
                    m = n - k
                    real = real + (xr[m] * er - xi[m] * ei) + (yr[m] * tr - yi[m] * ti)
                    imag = imag + (xr[m] * ei + xi[m] * er) + (yr[m] * ti + yi[m] * tr)
                z_spec[n, pl.ds(first, 8), :] = real
                z_spec[n, pl.ds(first + rows, 8), :] = imag
            return carry

        lax.fori_loop(0, rows // 8, one, 0)

    def correlate(spec, swapped):
        def one(tile, carry):
            left = first_lanes(8)
            zero = jnp.zeros((8, 128), f32)
            hr, hi = load(spec, tile, pairs)
            sr, si = load(swapped, tile, pairs)
            xr, xi = load(m_spec, tile, pairs)
            yr, yi = load(m_swap, tile, pairs)
            even = [
                (jnp.where(left, hr[k], sr[k]), jnp.where(left, hi[k], si[k]))
                for k in range(pairs)
            ]
            odd = [
                (
                    jnp.where(left, sr[k], hr[k - 1] if k else zero),
                    jnp.where(left, si[k], hi[k - 1] if k else zero),
                )
                for k in range(pairs)
            ]
            first = pl.multiple_of(tile * 8, 8)
            for n in range(pairs):
                real, imag = zero, zero
                for k in range(pairs - n):
                    er, ei = even[k]
                    tr, ti = odd[k]
                    m = n + k
                    real = real + (xr[m] * er + xi[m] * ei) + (yr[m] * tr + yi[m] * ti)
                    imag = imag + (xi[m] * er - xr[m] * ei) + (yi[m] * tr - yr[m] * ti)
                z_spec[n, pl.ds(first, 8), :] = real
                z_spec[n, pl.ds(first + rows, 8), :] = imag
            return carry

        lax.fori_loop(0, rows // 8, one, 0)

    def invert(unit, forward):
        def one(step, carry):
            block = jnp.concatenate([z_spec[2 * step], z_spec[2 * step + 1]], 1)
            field = split_dot(inv_ref[...], block)
            fields[2 * step + 1] = field[:, :128]
            fields[2 * step + 2] = field[:, 128:]
            return carry

        lax.fori_loop(0, pairs // 2, one, 0)

        def join(tile, carry):
            left = first_lanes(rows)
            here = swap(fields[tile + 1, rows:, :])
            if forward:
                there = swap(fields[tile, rows:, :])
                result = fields[tile + 1, :rows, :] + jnp.where(left, there, here)
            else:
                there = swap(fields[tile + 2, rows:, :])
                result = fields[tile + 1, :rows, :] - jnp.where(left, here, there)
            pack(unit, tile, result)
            return carry

        lax.fori_loop(0, pairs, join, 0)

    def pack_inputs(tile, carry):
        at = lanes(tile)
        pack(FILTER, tile, f_ref[:, at])
        pack(GATED, tile, k_ref[:, at].astype(f32) * v_ref[:, at].astype(f32))
        return carry

    lax.fori_loop(0, pairs, pack_inputs, 0)
    fields[0] = jnp.zeros((2 * rows, 128), f32)
    fields[pairs + 1] = jnp.zeros((2 * rows, 128), f32)

    pl.semaphore_wait(barrier, seq_count)
    send_all(FILTER)
    send_all(GATED)
    receive_all(FILTER)
    spectrum(FILTER, h_spec, h_swap)
    receive_all(GATED)
    spectrum(GATED, x_spec, x_swap)
    convolve()
    invert(CONV, True)
    send_all(CONV)
    receive_all(CONV)

    def activate(tile, carry):
        squares, crosses = carry
        at = lanes(tile)
        gated = k_ref[:, at].astype(f32) * v_ref[:, at].astype(f32)
        mixed = unpack(CONV, tile) + skip_ref[:, at] * gated
        mixed_ref[tile] = mixed
        activated = q_ref[:, at].astype(f32) * mixed
        scaled = g_ref[:, at].astype(f32) * norm_ref[:, at]
        return squares + activated * activated, crosses + scaled * activated

    nothing = jnp.zeros((rows, 128), f32)
    squares, crosses = lax.fori_loop(0, pairs, activate, (nothing, nothing))
    stat_send[0] = jnp.broadcast_to(jnp.sum(squares, axis=1, keepdims=True), (rows, 128))
    stat_send[1] = jnp.broadcast_to(jnp.sum(crosses, axis=1, keepdims=True), (rows, 128))
    stats = pltpu.make_async_remote_copy(
        src_ref=stat_send,
        dst_ref=stat_recv,
        send_sem=stat_sems.at[0],
        recv_sem=stat_sems.at[1],
        device_id={"chan": 1 - core},
        device_id_type=MESH,
    )
    stats.start()
    stats.wait()
    inverse_rms = lax.rsqrt((stat_send[0] + stat_recv[0]) / channel_total + epsilon_value)
    cross_mean = (stat_send[1] + stat_recv[1]) / channel_total
    cubed = inverse_rms * inverse_rms * inverse_rms * cross_mean

    def differentiate(tile, carry):
        at = lanes(tile)
        queries = q_ref[:, at].astype(f32)
        activated = queries * mixed_ref[tile]
        scaled = g_ref[:, at].astype(f32) * norm_ref[:, at]
        mix_grad = (inverse_rms * scaled - activated * cubed) * queries
        mix_ref[tile] = mix_grad
        pack(MIXGRAD, tile, mix_grad)
        return carry

    lax.fori_loop(0, pairs, differentiate, 0)
    send_all(MIXGRAD)

    def first_outputs(tile, carry):
        at = lanes(tile)
        mixed = mixed_ref[tile]
        activated = q_ref[:, at].astype(f32) * mixed
        scaled = g_ref[:, at].astype(f32) * norm_ref[:, at]
        out_ref[:, at] = (activated * inverse_rms * norm_ref[:, at]).astype(out_ref.dtype)
        qg_ref[:, at] = ((inverse_rms * scaled - activated * cubed) * mixed).astype(qg_ref.dtype)
        return carry

    lax.fori_loop(0, pairs, first_outputs, 0)
    receive_all(MIXGRAD)
    spectrum(MIXGRAD, m_spec, m_swap)
    correlate(h_spec, h_swap)
    invert(INPUT, False)
    send_all(INPUT)
    correlate(x_spec, x_swap)
    invert(FGRAD, False)
    send_all(FGRAD)
    receive_all(INPUT)

    def input_outputs(tile, carry):
        at = lanes(tile)
        gated_grad = unpack(INPUT, tile) + skip_ref[:, at] * mix_ref[tile]
        kg_ref[:, at] = (gated_grad * v_ref[:, at].astype(f32)).astype(kg_ref.dtype)
        vg_ref[:, at] = (gated_grad * k_ref[:, at].astype(f32)).astype(vg_ref.dtype)
        return carry

    lax.fori_loop(0, pairs, input_outputs, 0)
    receive_all(FGRAD)

    def filter_outputs(tile, carry):
        fg_ref[:, lanes(tile)] = unpack(FGRAD, tile)
        return carry

    lax.fori_loop(0, pairs, filter_outputs, 0)
    for unit in range(6):
        sent_all(unit)


def fast_body(query_proj, key_proj, value_proj, long_filter, skip_gain, norm_gain, out_grad):
    rows, width = query_proj.shape
    seq_count = lax.axis_size("seq")
    pairs = seq_count // 2
    forward, inverse = block_matrices(rows)
    vmem = pl.BlockSpec(memory_space=pltpu.VMEM)
    spec = pltpu.VMEM((pairs, 2 * rows, 128), jnp.float32)
    blocks = pltpu.VMEM((6, seq_count, rows // 2, 128), jnp.float32)
    held = pltpu.VMEM((pairs, rows, 128), jnp.float32)
    stat = pltpu.VMEM((2, rows, 128), jnp.float32)
    narrow = jax.ShapeDtypeStruct((rows, width), jnp.bfloat16)
    return pl.pallas_call(
        functools.partial(fast_kernel, seq_count),
        out_shape=(narrow,) * 4 + (jax.ShapeDtypeStruct((rows, width), jnp.float32),),
        in_specs=[vmem] * 9,
        out_specs=(vmem,) * 5,
        scratch_shapes=[
            blocks, blocks, spec, spec, spec, spec, spec, spec, spec,
            pltpu.VMEM((pairs + 2, 2 * rows, 128), jnp.float32),
            held, held, stat, stat,
            pltpu.SemaphoreType.DMA((6, seq_count)),
            pltpu.SemaphoreType.DMA((6, seq_count)),
            pltpu.SemaphoreType.DMA((2,)),
        ],
        compiler_params=pltpu.CompilerParams(
            collective_id=0, has_side_effects=True, vmem_limit_bytes=40 * 1024 * 1024
        ),
        cost_estimate=pl.CostEstimate(
            flops=2 * 10**9, bytes_accessed=4 * 10**6, transcendentals=rows * 128
        ),
    )(
        query_proj, key_proj, value_proj, long_filter,
        skip_gain[None, :], norm_gain[None, :], out_grad, forward, inverse,
    )


def choose_body(mesh, *arrays):
    rows, width = arrays[0].shape
    seq_count = mesh.shape["seq"]
    fits = width == 64 * seq_count and rows == 128 and seq_count % 4 == 0
    if fits and mesh.shape["chan"] == 2:
        return fast_body(*arrays)
    return wide_body(*arrays)


def solution(mesh):
    return jax.shard_map(
        functools.partial(choose_body, mesh),
        mesh=mesh,
        in_specs=(
            P("seq", "chan"),
            P("seq", "chan"),
            P("seq", "chan"),
            P("seq", "chan"),
            P("chan"),
            P("chan"),
            P("seq", "chan"),
        ),
        out_specs=(
            P("seq", "chan"),
            P("seq", "chan"),
            P("seq", "chan"),
            P("seq", "chan"),
            P("seq", "chan"),
        ),
        check_vma=False,
    )
```

```python
import functools
import math

import jax
import jax.numpy as jnp
import numpy as np
from jax import lax
from jax.experimental import pallas as pl
from jax.experimental.pallas import tpu as pltpu
from jax.sharding import PartitionSpec as P

exact_mode = lax.Precision.HIGHEST
epsilon_value = 1e-05


def dft_matrix(count, sign):
    indices = jnp.arange(count, dtype=jnp.int32)
    product = indices[:, None] * indices[None, :] % count
    angles = product.astype(jnp.float32) * (2.0 * math.pi / count)
    cosine = jnp.cos(angles)
    sine_part = sign * jnp.sin(angles)
    return jnp.stack([jnp.stack([cosine, -sine_part], 1), jnp.stack([sine_part, cosine], 1)], 0)


def rotate(field, angles):
    cos_part = jnp.cos(angles)
    sin_part = jnp.sin(angles)
    real_part = field[:, 0]
    imag_part = field[:, 1]
    return jnp.stack(
        [real_part * cos_part - imag_part * sin_part, real_part * sin_part + imag_part * cos_part],
        1,
    )


def prepare(signals, positions, length):
    angles = (positions.astype(jnp.float32) * (-math.pi / length))[..., None]
    cos_part = jnp.cos(angles)
    sin_part = jnp.sin(angles)
    real_in = signals[:, 0]
    real_part = jnp.stack([real_in, real_in * cos_part], 1)
    imag_part = jnp.stack([jnp.zeros_like(real_in), real_in * sin_part], 1)
    return jnp.stack([real_part, imag_part], 1)


def finish(field, positions, length):
    angles = (positions.astype(jnp.float32) * (math.pi / length))[..., None]
    second = rotate(field[:, :, 1], angles)
    return (field[:, :, 0] + second) / (2.0 * length)


def complex_product(first, second, conjugate):
    second_imag = -second[1] if conjugate else second[1]
    return jnp.stack(
        [
            first[0] * second[0] - first[1] * second_imag,
            first[0] * second_imag + first[1] * second[0],
        ],
        0,
    )


def wide_body(query_proj, key_proj, value_proj, long_filter, skip_gain, norm_gain, out_grad):
    tok_rows, chan_width = query_proj.shape
    seq_count = lax.axis_size("seq")
    seq_index = lax.axis_index("seq")
    length = tok_rows * seq_count
    channel_total = chan_width * lax.axis_size("chan")
    narrow_rows = tok_rows // seq_count
    forward_rows = dft_matrix(tok_rows, -1.0)
    inverse_rows = dft_matrix(tok_rows, 1.0)

    def block_places():
        offsets = seq_index * narrow_rows + jnp.arange(narrow_rows, dtype=jnp.int32)
        return jnp.arange(seq_count, dtype=jnp.int32)[:, None] * tok_rows + offsets[None, :]

    def channel_forward(signals):
        batch, width = (signals.shape[0], signals.shape[1])
        blocks = signals.reshape(batch, width, seq_count, narrow_rows, chan_width)
        spread = lax.all_to_all(blocks, "seq", split_axis=2, concat_axis=2, tiled=True)
        field = prepare(spread, block_places(), length)
        field = jnp.einsum(
            "pkqn,bqsnjc->bpskjc", dft_matrix(seq_count, -1.0), field, precision=exact_mode
        )
        offsets = seq_index * narrow_rows + jnp.arange(narrow_rows, dtype=jnp.int32)
        turns = jnp.arange(seq_count, dtype=jnp.int32)[:, None] * offsets[None, :] % length
        field = rotate(field, (turns.astype(jnp.float32) * (-2.0 * math.pi / length))[:, :, None])
        field = lax.all_to_all(field, "seq", split_axis=3, concat_axis=3, tiled=True)
        field = field.reshape(batch, 2, 2, tok_rows, chan_width)
        return jnp.einsum("pkqr,bqsrc->bpskc", forward_rows, field, precision=exact_mode)

    def channel_inverse(spectra, parts):
        batch = spectra.shape[0]
        field = jnp.einsum("pkqr,bqsrc->bpskc", inverse_rows, spectra, precision=exact_mode)
        turns = seq_index * jnp.arange(tok_rows, dtype=jnp.int32) % length
        field = rotate(field, (turns.astype(jnp.float32) * (2.0 * math.pi / length))[:, None])
        field = field.reshape(batch, 2, 2, seq_count, narrow_rows, chan_width)
        field = lax.all_to_all(field, "seq", split_axis=3, concat_axis=3, tiled=True)
        field = jnp.einsum(
            "pkqn,bqsnjc->bpskjc", dft_matrix(seq_count, 1.0), field, precision=exact_mode
        )
        result = finish(field, block_places(), length)[:, :parts]
        result = lax.all_to_all(result, "seq", split_axis=2, concat_axis=2, tiled=True)
        return result.reshape(batch, parts, tok_rows, chan_width)

    def transform(signals):
        return channel_forward(signals)

    def untransform(spectra, parts):
        return channel_inverse(spectra, parts)

    queries = query_proj.astype(jnp.float32)
    key_rows = key_proj.astype(jnp.float32)
    values = value_proj.astype(jnp.float32)
    gated_in = key_rows * values
    spectra = transform(jnp.stack([gated_in, long_filter], 0)[:, None])
    gated_spec = spectra[0]
    filter_spec = spectra[1]
    mixed_spec = complex_product(gated_spec, filter_spec, False)
    convolved = untransform(mixed_spec[None], 1)[0, 0]
    mixed = convolved + skip_gain[None, :] * gated_in
    activated = queries * mixed
    squares = lax.psum(jnp.sum(activated * activated, axis=1), "chan")
    inverse_rms = lax.rsqrt(squares / channel_total + epsilon_value)[:, None]
    block_out = (activated * inverse_rms * norm_gain[None, :]).astype(jnp.bfloat16)
    scaled_grad = out_grad.astype(jnp.float32) * norm_gain[None, :]
    cross_sum = lax.psum(jnp.sum(scaled_grad * activated, axis=1), "chan")
    cross_mean = (cross_sum / channel_total)[:, None]
    act_grad = inverse_rms * scaled_grad - activated * inverse_rms**3 * cross_mean
    query_grad = (act_grad * mixed).astype(jnp.bfloat16)
    mix_grad = act_grad * queries
    grad_spec = transform(mix_grad[None, None])[0]
    toward_input = complex_product(grad_spec, filter_spec, True)
    toward_filter = complex_product(grad_spec, gated_spec, True)
    results = untransform(jnp.stack([toward_input, toward_filter], 0), 1)
    input_part = results[0, 0]
    filter_grad = results[1, 0]
    gated_grad = input_part + skip_gain[None, :] * mix_grad
    key_grad = (gated_grad * values).astype(jnp.bfloat16)
    value_grad = (gated_grad * key_rows).astype(jnp.bfloat16)
    return (block_out, query_grad, key_grad, value_grad, filter_grad)


MESH = pl.DeviceIdType.MESH
GATED, FILTER, CONV, MIXGRAD, INPUT, FGRAD = range(6)


def split_matrix(matrix):
    matrix = jnp.asarray(matrix, jnp.float32)
    high = matrix.astype(jnp.bfloat16)
    low = (matrix - high.astype(jnp.float32)).astype(jnp.bfloat16)
    return jnp.concatenate([high, low, high], 1)


def block_matrices(rows):
    freqs = 2 * np.arange(rows) + 1
    places = np.arange(2 * rows)
    angles = np.pi / (2 * rows) * (freqs[:, None] * places[None, :] % (4 * rows))
    forward = np.concatenate([np.cos(angles), -np.sin(angles)], 0)[:, :rows]
    inverse = np.concatenate([np.cos(angles), -np.sin(angles)], 0).T / rows
    return split_matrix(forward), split_matrix(inverse)


def split_dot(matrix, values):
    high = values.astype(jnp.bfloat16)
    low = (values - high.astype(jnp.float32)).astype(jnp.bfloat16)
    return jnp.dot(
        matrix, jnp.concatenate([high, high, low], 0), preferred_element_type=jnp.float32
    )


def fast_kernel(
    seq_count,
    q_hbm, k_hbm, v_hbm, f_hbm, skip_hbm, norm_hbm, g_hbm, fwd_hbm, inv_hbm,
    out_hbm, qg_hbm, kg_hbm, vg_hbm, fg_hbm,
    out_ref, qg_ref, kg_ref, vg_ref, fg_ref,
    q_ref, k_ref, v_ref, f_ref, skip_ref, norm_ref, g_ref, fwd_ref, inv_ref,
    send, recv, h_spec, h_swap, x_spec, x_swap, m_spec, m_swap, z_spec, fields,
    even_ref, odd_ref, back_ref,
    mixed_ref, mix_ref, stat_send, stat_recv,
    send_sems, recv_sems, stat_sems, load_sems, store_sems,
):
    rows, width = q_ref.shape
    half = rows // 2
    pairs = seq_count // 2
    channel_total = 2 * width
    me = lax.axis_index("seq")
    core = lax.axis_index("chan")
    f32 = jnp.float32

    loads = [
        pltpu.make_async_copy(source, target, load_sems.at[place])
        for place, (source, target) in enumerate([
            (f_hbm, f_ref), (k_hbm, k_ref), (v_hbm, v_ref), (fwd_hbm, fwd_ref),
            (inv_hbm, inv_ref), (q_hbm, q_ref), (g_hbm, g_ref), (skip_hbm, skip_ref),
            (norm_hbm, norm_ref),
        ])
    ]
    for copy in loads:
        copy.start()
    stores = [
        pltpu.make_async_copy(source, target, store_sems.at[place])
        for place, (source, target) in enumerate([
            (out_ref, out_hbm), (qg_ref, qg_hbm), (kg_ref, kg_hbm), (vg_ref, vg_hbm),
            (fg_ref, fg_hbm),
        ])
    ]

    barrier = pltpu.get_barrier_semaphore()

    def greet(step, carry):
        peer = lax.rem(me + step, seq_count)
        pl.semaphore_signal(barrier, inc=1, device_id={"seq": peer}, device_id_type=MESH)
        return carry

    lax.fori_loop(1, seq_count, greet, 0)
    pl.semaphore_signal(barrier, inc=1, device_id={"chan": 1 - core}, device_id_type=MESH)

    def first_lanes(count):
        return lax.broadcasted_iota(jnp.int32, (count, 128), 1) < 64

    def swap(values):
        return pltpu.roll(values, 64, 1)

    def lanes(tile):
        return pl.ds(pl.multiple_of(tile * 128, 128), 128)

    def pack(unit, tile, values):
        top, bottom = values[:half], values[half:]
        left = first_lanes(half)
        send[unit, 2 * tile] = jnp.where(left, top, swap(bottom))
        send[unit, 2 * tile + 1] = jnp.where(left, swap(top), bottom)

    def unpack(unit, tile):
        first, second = recv[unit, 2 * tile], recv[unit, 2 * tile + 1]
        left = first_lanes(half)
        return jnp.concatenate(
            [jnp.where(left, first, swap(second)), jnp.where(left, swap(first), second)], 0
        )

    def remote(unit, src, dst, peer, send_slot, recv_slot):
        return pltpu.make_async_remote_copy(
            src_ref=send.at[unit, src],
            dst_ref=recv.at[unit, dst],
            send_sem=send_sems.at[unit, send_slot],
            recv_sem=recv_sems.at[unit, recv_slot],
            device_id={"seq": peer},
            device_id_type=MESH,
        )

    my_pair, my_side = me // 2, lax.rem(me, 2)

    def pair_at(step):
        odd_step = lax.rem(step, 2)
        flips = odd_step * ((step + 1) // 2) + (1 - odd_step) * (pairs // 2 + step // 2)
        pair, bit = 0, 1
        while bit < pairs:
            mine, flip = lax.rem(my_pair // bit, 2), lax.rem(flips // bit, 2)
            pair = pair + bit * (mine + flip - 2 * mine * flip)
            bit *= 2
        return pair

    def peers_at(step):
        return 2 * pair_at(step) + my_side, 2 * pair_at(step) + 1 - my_side

    neighbour = 2 * my_pair + 1 - my_side

    def send_all(unit):
        remote(unit, neighbour, me, neighbour, neighbour, me).start()

        def one(step, carry):
            for peer in peers_at(step):
                remote(unit, peer, me, peer, peer, me).start()
            return carry

        lax.fori_loop(0, pairs - 1, one, 0)
        recv[unit, me] = send[unit, me]

    def receive_each(unit, use, carry):
        remote(unit, neighbour, neighbour, neighbour, neighbour, neighbour).wait_recv()
        carry = use(my_pair, carry)

        def one(step, carry):
            for peer in peers_at(step):
                remote(unit, peer, peer, peer, peer, peer).wait_recv()
            return use(pair_at(step), carry)

        return lax.fori_loop(0, pairs - 1, one, carry)

    def sent_all(unit):
        remote(unit, neighbour, me, neighbour, neighbour, me).wait_send()

        def one(step, carry):
            for peer in peers_at(step):
                remote(unit, peer, me, peer, peer, me).wait_send()
            return carry

        lax.fori_loop(0, pairs - 1, one, 0)

    def transform(unit, spec, swapped, pair):
        field = split_dot(fwd_ref[...], unpack(unit, pair))
        spec[pair] = field
        swapped[pair] = swap(field)

    def clear_sums():
        def one(pair, carry):
            z_spec[pair] = jnp.zeros((2 * rows, 128), f32)
            return carry

        lax.fori_loop(0, pairs, one, 0)

    def lay_out_filter():
        def one(pair, carry):
            left = first_lanes(2 * rows)
            nothing = jnp.zeros((2 * rows, 128), f32)
            even_ref[pair] = nothing
            odd_ref[pair] = nothing
            back_ref[pair] = nothing
            here, there = h_spec[pair], h_swap[pair]
            before = lax.rem(pair + pairs - 1, pairs)
            started = jnp.where(pair > 0, 1.0, 0.0)
            even_ref[pairs + pair] = jnp.where(left, here, there)
            odd_ref[pairs + pair] = jnp.where(left, h_swap[before] * started, here)
            back_ref[pairs + pair] = jnp.where(left, there, h_spec[before] * started)
            return carry

        lax.fori_loop(0, pairs, one, 0)

    def add_products(spec, swapped, pair, forward):
        def one(tile, carry):
            first = pl.multiple_of(tile * 8, 8)
            real_rows, imag_rows = pl.ds(first, 8), pl.ds(first + rows, 8)
            xr, xi = spec[pair, real_rows, :], spec[pair, imag_rows, :]
            yr, yi = swapped[pair, real_rows, :], swapped[pair, imag_rows, :]
            for n in range(pairs):
                if forward:
                    place, cross = pairs + n - pair, odd_ref
                else:
                    place, cross = pairs + pair - n, back_ref
                er, ei = even_ref[place, real_rows, :], even_ref[place, imag_rows, :]
                tr, ti = cross[place, real_rows, :], cross[place, imag_rows, :]
                if forward:
                    real = (xr * er - xi * ei) + (yr * tr - yi * ti)
                    imag = (xr * ei + xi * er) + (yr * ti + yi * tr)
                else:
                    real = (xr * er + xi * ei) + (yr * tr + yi * ti)
                    imag = (xi * er - xr * ei) + (yi * tr - yr * ti)
                z_spec[n, real_rows, :] = z_spec[n, real_rows, :] + real
                z_spec[n, imag_rows, :] = z_spec[n, imag_rows, :] + imag
            return carry

        lax.fori_loop(0, rows // 8, one, 0)

    def load(ref, tile, count):
        first = pl.multiple_of(tile * 8, 8)
        real = [ref[k, pl.ds(first, 8), :] for k in range(count)]
        imag = [ref[k, pl.ds(first + rows, 8), :] for k in range(count)]
        return real, imag

    def correlate(spec, swapped):
        def one(tile, carry):
            left = first_lanes(8)
            zero = jnp.zeros((8, 128), f32)
            hr, hi = load(spec, tile, pairs)
            sr, si = load(swapped, tile, pairs)
            xr, xi = load(m_spec, tile, pairs)
            yr, yi = load(m_swap, tile, pairs)
            even = [
                (jnp.where(left, hr[k], sr[k]), jnp.where(left, hi[k], si[k]))
                for k in range(pairs)
            ]
            odd = [
                (
                    jnp.where(left, sr[k], hr[k - 1] if k else zero),
                    jnp.where(left, si[k], hi[k - 1] if k else zero),
                )
                for k in range(pairs)
            ]
            first = pl.multiple_of(tile * 8, 8)
            for n in range(pairs):
                real, imag = zero, zero
                for k in range(pairs - n):
                    er, ei = even[k]
                    tr, ti = odd[k]
                    m = n + k
                    real = real + (xr[m] * er + xi[m] * ei) + (yr[m] * tr + yi[m] * ti)
                    imag = imag + (xi[m] * er - xr[m] * ei) + (yi[m] * tr - yr[m] * ti)
                z_spec[n, pl.ds(first, 8), :] = real
                z_spec[n, pl.ds(first + rows, 8), :] = imag
            return carry

        lax.fori_loop(0, rows // 8, one, 0)

    def invert(unit, forward):
        def one(step, carry):
            block = jnp.concatenate([z_spec[2 * step], z_spec[2 * step + 1]], 1)
            field = split_dot(inv_ref[...], block)
            fields[2 * step + 1] = field[:, :128]
            fields[2 * step + 2] = field[:, 128:]
            return carry

        lax.fori_loop(0, pairs // 2, one, 0)

        def join(tile, carry):
            left = first_lanes(rows)
            here = swap(fields[tile + 1, rows:, :])
            if forward:
                there = swap(fields[tile, rows:, :])
                result = fields[tile + 1, :rows, :] + jnp.where(left, there, here)
            else:
                there = swap(fields[tile + 2, rows:, :])
                result = fields[tile + 1, :rows, :] - jnp.where(left, here, there)
            pack(unit, tile, result)
            return carry

        lax.fori_loop(0, pairs, join, 0)

    def pack_inputs(tile, carry):
        at = lanes(tile)
        pack(FILTER, tile, f_ref[:, at])
        pack(GATED, tile, k_ref[:, at].astype(f32) * v_ref[:, at].astype(f32))
        return carry

    for copy in loads[:3]:
        copy.wait()
    lax.fori_loop(0, pairs, pack_inputs, 0)
    fields[0] = jnp.zeros((2 * rows, 128), f32)
    fields[pairs + 1] = jnp.zeros((2 * rows, 128), f32)

    pl.semaphore_wait(barrier, seq_count)
    send_all(FILTER)
    send_all(GATED)
    for copy in loads[3:]:
        copy.wait()
    clear_sums()

    def take_filter(pair, carry):
        transform(FILTER, h_spec, h_swap, pair)
        return carry

    receive_each(FILTER, take_filter, 0)
    lay_out_filter()

    def take_gated(pair, carry):
        transform(GATED, x_spec, x_swap, pair)
        add_products(x_spec, x_swap, pair, True)
        return carry

    receive_each(GATED, take_gated, 0)
    invert(CONV, True)
    send_all(CONV)
    clear_sums()

    def activate(tile, carry):
        squares, crosses = carry
        at = lanes(tile)
        gated = k_ref[:, at].astype(f32) * v_ref[:, at].astype(f32)
        mixed = unpack(CONV, tile) + skip_ref[:, at] * gated
        mixed_ref[tile] = mixed
        activated = q_ref[:, at].astype(f32) * mixed
        scaled = g_ref[:, at].astype(f32) * norm_ref[:, at]
        return squares + activated * activated, crosses + scaled * activated

    nothing = jnp.zeros((rows, 128), f32)
    squares, crosses = receive_each(CONV, activate, (nothing, nothing))
    stat_send[0] = jnp.broadcast_to(jnp.sum(squares, axis=1, keepdims=True), (rows, 128))
    stat_send[1] = jnp.broadcast_to(jnp.sum(crosses, axis=1, keepdims=True), (rows, 128))
    stats = pltpu.make_async_remote_copy(
        src_ref=stat_send,
        dst_ref=stat_recv,
        send_sem=stat_sems.at[0],
        recv_sem=stat_sems.at[1],
        device_id={"chan": 1 - core},
        device_id_type=MESH,
    )
    stats.start()
    stats.wait()
    inverse_rms = lax.rsqrt((stat_send[0] + stat_recv[0]) / channel_total + epsilon_value)
    cross_mean = (stat_send[1] + stat_recv[1]) / channel_total
    cubed = inverse_rms * inverse_rms * inverse_rms * cross_mean

    def differentiate(tile, carry):
        at = lanes(tile)
        queries = q_ref[:, at].astype(f32)
        activated = queries * mixed_ref[tile]
        scaled = g_ref[:, at].astype(f32) * norm_ref[:, at]
        mix_grad = (inverse_rms * scaled - activated * cubed) * queries
        mix_ref[tile] = mix_grad
        pack(MIXGRAD, tile, mix_grad)
        return carry

    lax.fori_loop(0, pairs, differentiate, 0)
    send_all(MIXGRAD)

    def first_outputs(tile, carry):
        at = lanes(tile)
        mixed = mixed_ref[tile]
        activated = q_ref[:, at].astype(f32) * mixed
        scaled = g_ref[:, at].astype(f32) * norm_ref[:, at]
        out_ref[:, at] = (activated * inverse_rms * norm_ref[:, at]).astype(out_ref.dtype)
        qg_ref[:, at] = ((inverse_rms * scaled - activated * cubed) * mixed).astype(qg_ref.dtype)
        return carry

    lax.fori_loop(0, pairs, first_outputs, 0)
    for copy in stores[:2]:
        copy.start()

    def take_grad(pair, carry):
        transform(MIXGRAD, m_spec, m_swap, pair)
        add_products(m_spec, m_swap, pair, False)
        return carry

    receive_each(MIXGRAD, take_grad, 0)
    invert(INPUT, False)
    send_all(INPUT)
    correlate(x_spec, x_swap)
    invert(FGRAD, False)
    send_all(FGRAD)
    def input_outputs(tile, carry):
        at = lanes(tile)
        gated_grad = unpack(INPUT, tile) + skip_ref[:, at] * mix_ref[tile]
        kg_ref[:, at] = (gated_grad * v_ref[:, at].astype(f32)).astype(kg_ref.dtype)
        vg_ref[:, at] = (gated_grad * k_ref[:, at].astype(f32)).astype(vg_ref.dtype)
        return carry

    receive_each(INPUT, input_outputs, 0)
    for copy in stores[2:4]:
        copy.start()

    def filter_outputs(tile, carry):
        fg_ref[:, lanes(tile)] = unpack(FGRAD, tile)
        return carry

    receive_each(FGRAD, filter_outputs, 0)
    stores[4].start()
    for unit in range(6):
        sent_all(unit)
    for copy in stores:
        copy.wait()


def write_kernel(count, *refs):
    held, written, sems = refs[:count], refs[count:2 * count], refs[2 * count]
    copies = [
        pltpu.make_async_copy(source, target, sems.at[place])
        for place, (source, target) in enumerate(zip(held, written))
    ]
    for copy in copies:
        copy.start()
    for copy in copies:
        copy.wait()


def fast_body(query_proj, key_proj, value_proj, long_filter, skip_gain, norm_gain, out_grad):
    rows, width = query_proj.shape
    seq_count = lax.axis_size("seq")
    pairs = seq_count // 2
    forward, inverse = block_matrices(rows)
    operands = (
        query_proj, key_proj, value_proj, long_filter,
        skip_gain[None, :], norm_gain[None, :], out_grad, forward, inverse,
    )
    anywhere = pl.BlockSpec(memory_space=pltpu.HBM)
    spec = pltpu.VMEM((pairs, 2 * rows, 128), jnp.float32)
    laid = pltpu.VMEM((2 * pairs, 2 * rows, 128), jnp.float32)
    blocks = pltpu.VMEM((6, seq_count, rows // 2, 128), jnp.float32)
    held = pltpu.VMEM((pairs, rows, 128), jnp.float32)
    stat = pltpu.VMEM((2, rows, 128), jnp.float32)
    narrow = jax.ShapeDtypeStruct((rows, width), jnp.bfloat16)
    shapes = (narrow,) * 4 + (jax.ShapeDtypeStruct((rows, width), jnp.float32),)
    results = pl.pallas_call(
        functools.partial(fast_kernel, seq_count),
        out_shape=shapes,
        in_specs=[anywhere] * len(operands),
        out_specs=(anywhere,) * 5,
        scratch_shapes=[pltpu.VMEM(one.shape, one.dtype) for one in shapes + operands] + [
            blocks, blocks, spec, spec, spec, spec, spec, spec, spec,
            pltpu.VMEM((pairs + 2, 2 * rows, 128), jnp.float32),
            laid, laid, laid,
            held, held, stat, stat,
            pltpu.SemaphoreType.DMA((6, seq_count)),
            pltpu.SemaphoreType.DMA((6, seq_count)),
            pltpu.SemaphoreType.DMA((2,)),
            pltpu.SemaphoreType.DMA((len(operands),)),
            pltpu.SemaphoreType.DMA((len(shapes),)),
        ],
        compiler_params=pltpu.CompilerParams(
            collective_id=0, has_side_effects=True, vmem_limit_bytes=62 * 1024 * 1024
        ),
        cost_estimate=pl.CostEstimate(
            flops=2 * 10**9, bytes_accessed=4 * 10**6, transcendentals=rows * 128
        ),
    )(*operands)
    return pl.pallas_call(
        functools.partial(write_kernel, len(shapes)),
        out_shape=shapes,
        in_specs=[anywhere] * len(shapes),
        out_specs=(anywhere,) * len(shapes),
        scratch_shapes=[pltpu.SemaphoreType.DMA((len(shapes),))],
        compiler_params=pltpu.CompilerParams(vmem_limit_bytes=62 * 1024 * 1024),
    )(*results)


def choose_body(mesh, *arrays):
    rows, width = arrays[0].shape
    seq_count = mesh.shape["seq"]
    power = seq_count & (seq_count - 1) == 0
    fits = width == 64 * seq_count and rows == 128 and seq_count >= 4 and power
    if fits and mesh.shape["chan"] == 2:
        return fast_body(*arrays)
    return wide_body(*arrays)


def solution(mesh):
    return jax.shard_map(
        functools.partial(choose_body, mesh),
        mesh=mesh,
        in_specs=(
            P("seq", "chan"),
            P("seq", "chan"),
            P("seq", "chan"),
            P("seq", "chan"),
            P("chan"),
            P("chan"),
            P("seq", "chan"),
        ),
        out_specs=(
            P("seq", "chan"),
            P("seq", "chan"),
            P("seq", "chan"),
            P("seq", "chan"),
            P("seq", "chan"),
        ),
        check_vma=False,
    )
```

```python
import functools
import math

import jax
import jax.numpy as jnp
import numpy as np
from jax import lax
from jax.experimental import pallas as pl
from jax.experimental.pallas import tpu as pltpu
from jax.sharding import PartitionSpec as P

exact_mode = lax.Precision.HIGHEST
epsilon_value = 1e-05


def dft_matrix(count, sign):
    indices = jnp.arange(count, dtype=jnp.int32)
    product = indices[:, None] * indices[None, :] % count
    angles = product.astype(jnp.float32) * (2.0 * math.pi / count)
    cosine = jnp.cos(angles)
    sine_part = sign * jnp.sin(angles)
    return jnp.stack([jnp.stack([cosine, -sine_part], 1), jnp.stack([sine_part, cosine], 1)], 0)


def rotate(field, angles):
    cos_part = jnp.cos(angles)
    sin_part = jnp.sin(angles)
    real_part = field[:, 0]
    imag_part = field[:, 1]
    return jnp.stack(
        [real_part * cos_part - imag_part * sin_part, real_part * sin_part + imag_part * cos_part],
        1,
    )


def prepare(signals, positions, length):
    angles = (positions.astype(jnp.float32) * (-math.pi / length))[..., None]
    cos_part = jnp.cos(angles)
    sin_part = jnp.sin(angles)
    real_in = signals[:, 0]
    real_part = jnp.stack([real_in, real_in * cos_part], 1)
    imag_part = jnp.stack([jnp.zeros_like(real_in), real_in * sin_part], 1)
    return jnp.stack([real_part, imag_part], 1)


def finish(field, positions, length):
    angles = (positions.astype(jnp.float32) * (math.pi / length))[..., None]
    second = rotate(field[:, :, 1], angles)
    return (field[:, :, 0] + second) / (2.0 * length)


def complex_product(first, second, conjugate):
    second_imag = -second[1] if conjugate else second[1]
    return jnp.stack(
        [
            first[0] * second[0] - first[1] * second_imag,
            first[0] * second_imag + first[1] * second[0],
        ],
        0,
    )


def wide_body(query_proj, key_proj, value_proj, long_filter, skip_gain, norm_gain, out_grad):
    tok_rows, chan_width = query_proj.shape
    seq_count = lax.axis_size("seq")
    seq_index = lax.axis_index("seq")
    length = tok_rows * seq_count
    channel_total = chan_width * lax.axis_size("chan")
    narrow_rows = tok_rows // seq_count
    forward_rows = dft_matrix(tok_rows, -1.0)
    inverse_rows = dft_matrix(tok_rows, 1.0)

    def block_places():
        offsets = seq_index * narrow_rows + jnp.arange(narrow_rows, dtype=jnp.int32)
        return jnp.arange(seq_count, dtype=jnp.int32)[:, None] * tok_rows + offsets[None, :]

    def channel_forward(signals):
        batch, width = (signals.shape[0], signals.shape[1])
        blocks = signals.reshape(batch, width, seq_count, narrow_rows, chan_width)
        spread = lax.all_to_all(blocks, "seq", split_axis=2, concat_axis=2, tiled=True)
        field = prepare(spread, block_places(), length)
        field = jnp.einsum(
            "pkqn,bqsnjc->bpskjc", dft_matrix(seq_count, -1.0), field, precision=exact_mode
        )
        offsets = seq_index * narrow_rows + jnp.arange(narrow_rows, dtype=jnp.int32)
        turns = jnp.arange(seq_count, dtype=jnp.int32)[:, None] * offsets[None, :] % length
        field = rotate(field, (turns.astype(jnp.float32) * (-2.0 * math.pi / length))[:, :, None])
        field = lax.all_to_all(field, "seq", split_axis=3, concat_axis=3, tiled=True)
        field = field.reshape(batch, 2, 2, tok_rows, chan_width)
        return jnp.einsum("pkqr,bqsrc->bpskc", forward_rows, field, precision=exact_mode)

    def channel_inverse(spectra, parts):
        batch = spectra.shape[0]
        field = jnp.einsum("pkqr,bqsrc->bpskc", inverse_rows, spectra, precision=exact_mode)
        turns = seq_index * jnp.arange(tok_rows, dtype=jnp.int32) % length
        field = rotate(field, (turns.astype(jnp.float32) * (2.0 * math.pi / length))[:, None])
        field = field.reshape(batch, 2, 2, seq_count, narrow_rows, chan_width)
        field = lax.all_to_all(field, "seq", split_axis=3, concat_axis=3, tiled=True)
        field = jnp.einsum(
            "pkqn,bqsnjc->bpskjc", dft_matrix(seq_count, 1.0), field, precision=exact_mode
        )
        result = finish(field, block_places(), length)[:, :parts]
        result = lax.all_to_all(result, "seq", split_axis=2, concat_axis=2, tiled=True)
        return result.reshape(batch, parts, tok_rows, chan_width)

    def transform(signals):
        return channel_forward(signals)

    def untransform(spectra, parts):
        return channel_inverse(spectra, parts)

    queries = query_proj.astype(jnp.float32)
    key_rows = key_proj.astype(jnp.float32)
    values = value_proj.astype(jnp.float32)
    gated_in = key_rows * values
    spectra = transform(jnp.stack([gated_in, long_filter], 0)[:, None])
    gated_spec = spectra[0]
    filter_spec = spectra[1]
    mixed_spec = complex_product(gated_spec, filter_spec, False)
    convolved = untransform(mixed_spec[None], 1)[0, 0]
    mixed = convolved + skip_gain[None, :] * gated_in
    activated = queries * mixed
    squares = lax.psum(jnp.sum(activated * activated, axis=1), "chan")
    inverse_rms = lax.rsqrt(squares / channel_total + epsilon_value)[:, None]
    block_out = (activated * inverse_rms * norm_gain[None, :]).astype(jnp.bfloat16)
    scaled_grad = out_grad.astype(jnp.float32) * norm_gain[None, :]
    cross_sum = lax.psum(jnp.sum(scaled_grad * activated, axis=1), "chan")
    cross_mean = (cross_sum / channel_total)[:, None]
    act_grad = inverse_rms * scaled_grad - activated * inverse_rms**3 * cross_mean
    query_grad = (act_grad * mixed).astype(jnp.bfloat16)
    mix_grad = act_grad * queries
    grad_spec = transform(mix_grad[None, None])[0]
    toward_input = complex_product(grad_spec, filter_spec, True)
    toward_filter = complex_product(grad_spec, gated_spec, True)
    results = untransform(jnp.stack([toward_input, toward_filter], 0), 1)
    input_part = results[0, 0]
    filter_grad = results[1, 0]
    gated_grad = input_part + skip_gain[None, :] * mix_grad
    key_grad = (gated_grad * values).astype(jnp.bfloat16)
    value_grad = (gated_grad * key_rows).astype(jnp.bfloat16)
    return (block_out, query_grad, key_grad, value_grad, filter_grad)


MESH = pl.DeviceIdType.MESH
GATED, FILTER, CONV, MIXGRAD, INPUT, FGRAD = range(6)


def split_matrix(matrix):
    matrix = jnp.asarray(matrix, jnp.float32)
    high = matrix.astype(jnp.bfloat16)
    low = (matrix - high.astype(jnp.float32)).astype(jnp.bfloat16)
    return jnp.concatenate([high, low, high], 1)


def block_matrices(rows):
    freqs = 2 * np.arange(rows) + 1
    places = np.arange(2 * rows)
    angles = np.pi / (2 * rows) * (freqs[:, None] * places[None, :] % (4 * rows))
    forward = np.concatenate([np.cos(angles), -np.sin(angles)], 0)[:, :rows]
    inverse = np.concatenate([np.cos(angles), -np.sin(angles)], 0).T / rows
    return split_matrix(forward), split_matrix(inverse)


def split_dot(matrix, values):
    high = values.astype(jnp.bfloat16)
    low = (values - high.astype(jnp.float32)).astype(jnp.bfloat16)
    return jnp.dot(
        matrix, jnp.concatenate([high, high, low], 0), preferred_element_type=jnp.float32
    )


def fast_kernel(
    seq_count,
    q_hbm, k_hbm, v_hbm, f_hbm, skip_hbm, norm_hbm, g_hbm, fwd_hbm, inv_hbm,
    out_hbm, qg_hbm, kg_hbm, vg_hbm, fg_hbm,
    out_ref, qg_ref, kg_ref, vg_ref, fg_ref,
    q_ref, k_ref, v_ref, f_ref, skip_ref, norm_ref, g_ref, fwd_ref, inv_ref,
    send, recv, h_spec, h_swap, x_spec, x_swap, m_spec, m_swap, z_spec, fields,
    even_ref, odd_ref, back_ref,
    mixed_ref, mix_ref, stat_send, stat_recv,
    send_sems, recv_sems, stat_sems, load_sems, store_sems,
):
    rows, width = q_ref.shape
    half = rows // 2
    pairs = seq_count // 2
    channel_total = 2 * width
    me = lax.axis_index("seq")
    core = lax.axis_index("chan")
    f32 = jnp.float32

    loads = [
        pltpu.make_async_copy(source, target, load_sems.at[place])
        for place, (source, target) in enumerate([
            (f_hbm, f_ref), (k_hbm, k_ref), (v_hbm, v_ref), (fwd_hbm, fwd_ref),
            (inv_hbm, inv_ref), (q_hbm, q_ref), (g_hbm, g_ref), (skip_hbm, skip_ref),
            (norm_hbm, norm_ref),
        ])
    ]
    for copy in loads:
        copy.start()
    stores = [
        pltpu.make_async_copy(source, target, store_sems.at[place])
        for place, (source, target) in enumerate([
            (out_ref, out_hbm), (qg_ref, qg_hbm), (kg_ref, kg_hbm), (vg_ref, vg_hbm),
            (fg_ref, fg_hbm),
        ])
    ]

    barrier = pltpu.get_barrier_semaphore()

    def greet(step, carry):
        peer = lax.rem(me + step, seq_count)
        pl.semaphore_signal(barrier, inc=1, device_id={"seq": peer}, device_id_type=MESH)
        return carry

    lax.fori_loop(1, seq_count, greet, 0)
    pl.semaphore_signal(barrier, inc=1, device_id={"chan": 1 - core}, device_id_type=MESH)

    def first_lanes(count):
        return lax.broadcasted_iota(jnp.int32, (count, 128), 1) < 64

    def swap(values):
        return pltpu.roll(values, 64, 1)

    def lanes(tile):
        return pl.ds(pl.multiple_of(tile * 128, 128), 128)

    def pack(unit, tile, values):
        top, bottom = values[:half], values[half:]
        left = first_lanes(half)
        send[unit, 2 * tile] = jnp.where(left, top, swap(bottom))
        send[unit, 2 * tile + 1] = jnp.where(left, swap(top), bottom)

    def unpack(unit, tile):
        first, second = recv[unit, 2 * tile], recv[unit, 2 * tile + 1]
        left = first_lanes(half)
        return jnp.concatenate(
            [jnp.where(left, first, swap(second)), jnp.where(left, swap(first), second)], 0
        )

    def remote(unit, src, dst, peer, send_slot, recv_slot):
        return pltpu.make_async_remote_copy(
            src_ref=send.at[unit, src],
            dst_ref=recv.at[unit, dst],
            send_sem=send_sems.at[unit, send_slot],
            recv_sem=recv_sems.at[unit, recv_slot],
            device_id={"seq": peer},
            device_id_type=MESH,
        )

    my_pair, my_side = me // 2, lax.rem(me, 2)

    def pair_at(flips):
        pair, bit = 0, 1
        while bit < pairs:
            mine, flip = lax.rem(my_pair // bit, 2), lax.rem(flips // bit, 2)
            pair = pair + bit * (mine + flip - 2 * mine * flip)
            bit *= 2
        return pair

    odd_plane = lax.rem(my_pair // 2, 2)

    def send_flips(step):
        later, turn = step // 4, lax.rem(step, 4)
        plane = odd_plane + later - 2 * odd_plane * later
        return 4 * (1 - lax.rem(turn, 2)) + 2 * plane + turn // 2

    def receive_flips(step):
        turn = step // 2
        return 4 * (1 - lax.rem(turn, 2)) + 2 * lax.rem(step, 2) + turn // 2

    def for_peers(flips, use):
        pair = pair_at(flips)
        use(2 * pair + 1 - my_side)

        @pl.when(flips > 0)
        def _():
            use(2 * pair + my_side)

        return pair

    def send_all(unit):
        recv[unit, me] = send[unit, me]

        def one(step, carry):
            for_peers(
                send_flips(step),
                lambda peer: remote(unit, peer, me, peer, peer, me).start(),
            )
            return carry

        lax.fori_loop(0, pairs, one, 0)

    def receive_each(unit, use, carry):
        def one(step, carry):
            pair = for_peers(
                receive_flips(step),
                lambda peer: remote(unit, peer, peer, peer, peer, peer).wait_recv(),
            )
            return use(pair, carry)

        return lax.fori_loop(0, pairs, one, carry)

    def sent_all(unit):
        def one(step, carry):
            for_peers(
                send_flips(step),
                lambda peer: remote(unit, peer, me, peer, peer, me).wait_send(),
            )
            return carry

        lax.fori_loop(0, pairs, one, 0)

    def transform(unit, spec, swapped, pair):
        field = split_dot(fwd_ref[...], unpack(unit, pair))
        spec[pair] = field
        swapped[pair] = swap(field)

    def clear_sums():
        def one(pair, carry):
            z_spec[pair] = jnp.zeros((2 * rows, 128), f32)
            return carry

        lax.fori_loop(0, pairs, one, 0)

    def lay_out_filter():
        def one(pair, carry):
            left = first_lanes(2 * rows)
            nothing = jnp.zeros((2 * rows, 128), f32)
            even_ref[pair] = nothing
            odd_ref[pair] = nothing
            back_ref[pair] = nothing
            here, there = h_spec[pair], h_swap[pair]
            before = lax.rem(pair + pairs - 1, pairs)
            started = jnp.where(pair > 0, 1.0, 0.0)
            even_ref[pairs + pair] = jnp.where(left, here, there)
            odd_ref[pairs + pair] = jnp.where(left, h_swap[before] * started, here)
            back_ref[pairs + pair] = jnp.where(left, there, h_spec[before] * started)
            return carry

        lax.fori_loop(0, pairs, one, 0)

    def add_products(spec, swapped, pair, forward):
        def one(tile, carry):
            first = pl.multiple_of(tile * 8, 8)
            real_rows, imag_rows = pl.ds(first, 8), pl.ds(first + rows, 8)
            xr, xi = spec[pair, real_rows, :], spec[pair, imag_rows, :]
            yr, yi = swapped[pair, real_rows, :], swapped[pair, imag_rows, :]
            for n in range(pairs):
                if forward:
                    place, cross = pairs + n - pair, odd_ref
                else:
                    place, cross = pairs + pair - n, back_ref
                er, ei = even_ref[place, real_rows, :], even_ref[place, imag_rows, :]
                tr, ti = cross[place, real_rows, :], cross[place, imag_rows, :]
                if forward:
                    real = (xr * er - xi * ei) + (yr * tr - yi * ti)
                    imag = (xr * ei + xi * er) + (yr * ti + yi * tr)
                else:
                    real = (xr * er + xi * ei) + (yr * tr + yi * ti)
                    imag = (xi * er - xr * ei) + (yi * tr - yr * ti)
                z_spec[n, real_rows, :] = z_spec[n, real_rows, :] + real
                z_spec[n, imag_rows, :] = z_spec[n, imag_rows, :] + imag
            return carry

        lax.fori_loop(0, rows // 8, one, 0)

    def load(ref, tile, count):
        first = pl.multiple_of(tile * 8, 8)
        real = [ref[k, pl.ds(first, 8), :] for k in range(count)]
        imag = [ref[k, pl.ds(first + rows, 8), :] for k in range(count)]
        return real, imag

    def correlate(spec, swapped):
        def one(tile, carry):
            left = first_lanes(8)
            zero = jnp.zeros((8, 128), f32)
            hr, hi = load(spec, tile, pairs)
            sr, si = load(swapped, tile, pairs)
            xr, xi = load(m_spec, tile, pairs)
            yr, yi = load(m_swap, tile, pairs)
            even = [
                (jnp.where(left, hr[k], sr[k]), jnp.where(left, hi[k], si[k]))
                for k in range(pairs)
            ]
            odd = [
                (
                    jnp.where(left, sr[k], hr[k - 1] if k else zero),
                    jnp.where(left, si[k], hi[k - 1] if k else zero),
                )
                for k in range(pairs)
            ]
            first = pl.multiple_of(tile * 8, 8)
            for n in range(pairs):
                real, imag = zero, zero
                for k in range(pairs - n):
                    er, ei = even[k]
                    tr, ti = odd[k]
                    m = n + k
                    real = real + (xr[m] * er + xi[m] * ei) + (yr[m] * tr + yi[m] * ti)
                    imag = imag + (xi[m] * er - xr[m] * ei) + (yi[m] * tr - yr[m] * ti)
                z_spec[n, pl.ds(first, 8), :] = real
                z_spec[n, pl.ds(first + rows, 8), :] = imag
            return carry

        lax.fori_loop(0, rows // 8, one, 0)

    def invert(unit, forward):
        def one(step, carry):
            block = jnp.concatenate([z_spec[2 * step], z_spec[2 * step + 1]], 1)
            field = split_dot(inv_ref[...], block)
            fields[2 * step + 1] = field[:, :128]
            fields[2 * step + 2] = field[:, 128:]
            return carry

        lax.fori_loop(0, pairs // 2, one, 0)

        def join(tile, carry):
            left = first_lanes(rows)
            here = swap(fields[tile + 1, rows:, :])
            if forward:
                there = swap(fields[tile, rows:, :])
                result = fields[tile + 1, :rows, :] + jnp.where(left, there, here)
            else:
                there = swap(fields[tile + 2, rows:, :])
                result = fields[tile + 1, :rows, :] - jnp.where(left, here, there)
            pack(unit, tile, result)
            return carry

        lax.fori_loop(0, pairs, join, 0)

    def pack_inputs(tile, carry):
        at = lanes(tile)
        pack(FILTER, tile, f_ref[:, at])
        pack(GATED, tile, k_ref[:, at].astype(f32) * v_ref[:, at].astype(f32))
        return carry

    for copy in loads[:3]:
        copy.wait()
    lax.fori_loop(0, pairs, pack_inputs, 0)
    fields[0] = jnp.zeros((2 * rows, 128), f32)
    fields[pairs + 1] = jnp.zeros((2 * rows, 128), f32)

    pl.semaphore_wait(barrier, seq_count)
    send_all(FILTER)
    send_all(GATED)
    for copy in loads[3:]:
        copy.wait()
    clear_sums()

    def take_filter(pair, carry):
        transform(FILTER, h_spec, h_swap, pair)
        return carry

    receive_each(FILTER, take_filter, 0)
    lay_out_filter()

    def take_gated(pair, carry):
        transform(GATED, x_spec, x_swap, pair)
        add_products(x_spec, x_swap, pair, True)
        return carry

    receive_each(GATED, take_gated, 0)
    invert(CONV, True)
    send_all(CONV)
    clear_sums()

    def activate(tile, carry):
        squares, crosses = carry
        at = lanes(tile)
        gated = k_ref[:, at].astype(f32) * v_ref[:, at].astype(f32)
        mixed = unpack(CONV, tile) + skip_ref[:, at] * gated
        mixed_ref[tile] = mixed
        activated = q_ref[:, at].astype(f32) * mixed
        scaled = g_ref[:, at].astype(f32) * norm_ref[:, at]
        return squares + activated * activated, crosses + scaled * activated

    nothing = jnp.zeros((rows, 128), f32)
    squares, crosses = receive_each(CONV, activate, (nothing, nothing))
    stat_send[0] = jnp.broadcast_to(jnp.sum(squares, axis=1, keepdims=True), (rows, 128))
    stat_send[1] = jnp.broadcast_to(jnp.sum(crosses, axis=1, keepdims=True), (rows, 128))
    stats = pltpu.make_async_remote_copy(
        src_ref=stat_send,
        dst_ref=stat_recv,
        send_sem=stat_sems.at[0],
        recv_sem=stat_sems.at[1],
        device_id={"chan": 1 - core},
        device_id_type=MESH,
    )
    stats.start()
    stats.wait()
    inverse_rms = lax.rsqrt((stat_send[0] + stat_recv[0]) / channel_total + epsilon_value)
    cross_mean = (stat_send[1] + stat_recv[1]) / channel_total
    cubed = inverse_rms * inverse_rms * inverse_rms * cross_mean

    def differentiate(tile, carry):
        at = lanes(tile)
        queries = q_ref[:, at].astype(f32)
        activated = queries * mixed_ref[tile]
        scaled = g_ref[:, at].astype(f32) * norm_ref[:, at]
        mix_grad = (inverse_rms * scaled - activated * cubed) * queries
        mix_ref[tile] = mix_grad
        pack(MIXGRAD, tile, mix_grad)
        return carry

    lax.fori_loop(0, pairs, differentiate, 0)
    send_all(MIXGRAD)

    def first_outputs(tile, carry):
        at = lanes(tile)
        mixed = mixed_ref[tile]
        activated = q_ref[:, at].astype(f32) * mixed
        scaled = g_ref[:, at].astype(f32) * norm_ref[:, at]
        out_ref[:, at] = (activated * inverse_rms * norm_ref[:, at]).astype(out_ref.dtype)
        qg_ref[:, at] = ((inverse_rms * scaled - activated * cubed) * mixed).astype(qg_ref.dtype)
        return carry

    lax.fori_loop(0, pairs, first_outputs, 0)
    for copy in stores[:2]:
        copy.start()

    def take_grad(pair, carry):
        transform(MIXGRAD, m_spec, m_swap, pair)
        add_products(m_spec, m_swap, pair, False)
        return carry

    receive_each(MIXGRAD, take_grad, 0)
    invert(INPUT, False)
    send_all(INPUT)
    correlate(x_spec, x_swap)
    invert(FGRAD, False)
    send_all(FGRAD)
    def input_outputs(tile, carry):
        at = lanes(tile)
        gated_grad = unpack(INPUT, tile) + skip_ref[:, at] * mix_ref[tile]
        kg_ref[:, at] = (gated_grad * v_ref[:, at].astype(f32)).astype(kg_ref.dtype)
        vg_ref[:, at] = (gated_grad * k_ref[:, at].astype(f32)).astype(vg_ref.dtype)
        return carry

    receive_each(INPUT, input_outputs, 0)
    for copy in stores[2:4]:
        copy.start()

    def filter_outputs(tile, carry):
        fg_ref[:, lanes(tile)] = unpack(FGRAD, tile)
        return carry

    receive_each(FGRAD, filter_outputs, 0)
    stores[4].start()
    for unit in range(6):
        sent_all(unit)
    for copy in stores:
        copy.wait()


def write_kernel(count, *refs):
    read, written, held = (refs[count * part:count * part + count] for part in range(3))
    sems = refs[3 * count]
    inward = [
        pltpu.make_async_copy(read[place], held[place], sems.at[0, place])
        for place in range(count)
    ]
    outward = [
        pltpu.make_async_copy(held[place], written[place], sems.at[1, place])
        for place in range(count)
    ]
    for copy in inward:
        copy.start()
    for first, second in zip(inward, outward):
        first.wait()
        second.start()
    for copy in outward:
        copy.wait()


def fast_body(query_proj, key_proj, value_proj, long_filter, skip_gain, norm_gain, out_grad):
    rows, width = query_proj.shape
    seq_count = lax.axis_size("seq")
    pairs = seq_count // 2
    forward, inverse = block_matrices(rows)
    operands = (
        query_proj, key_proj, value_proj, long_filter,
        skip_gain[None, :], norm_gain[None, :], out_grad, forward, inverse,
    )
    anywhere = pl.BlockSpec(memory_space=pltpu.HBM)
    spec = pltpu.VMEM((pairs, 2 * rows, 128), jnp.float32)
    laid = pltpu.VMEM((2 * pairs, 2 * rows, 128), jnp.float32)
    blocks = pltpu.VMEM((6, seq_count, rows // 2, 128), jnp.float32)
    held = pltpu.VMEM((pairs, rows, 128), jnp.float32)
    stat = pltpu.VMEM((2, rows, 128), jnp.float32)
    narrow = jax.ShapeDtypeStruct((rows, width), jnp.bfloat16)
    shapes = (narrow,) * 4 + (jax.ShapeDtypeStruct((rows, width), jnp.float32),)
    results = pl.pallas_call(
        functools.partial(fast_kernel, seq_count),
        out_shape=shapes,
        in_specs=[anywhere] * len(operands),
        out_specs=(anywhere,) * 5,
        scratch_shapes=[pltpu.VMEM(one.shape, one.dtype) for one in shapes + operands] + [
            blocks, blocks, spec, spec, spec, spec, spec, spec, spec,
            pltpu.VMEM((pairs + 2, 2 * rows, 128), jnp.float32),
            laid, laid, laid,
            held, held, stat, stat,
            pltpu.SemaphoreType.DMA((6, seq_count)),
            pltpu.SemaphoreType.DMA((6, seq_count)),
            pltpu.SemaphoreType.DMA((2,)),
            pltpu.SemaphoreType.DMA((len(operands),)),
            pltpu.SemaphoreType.DMA((len(shapes),)),
        ],
        compiler_params=pltpu.CompilerParams(
            collective_id=0, has_side_effects=True, vmem_limit_bytes=62 * 1024 * 1024
        ),
        cost_estimate=pl.CostEstimate(
            flops=2 * 10**9, bytes_accessed=4 * 10**6, transcendentals=rows * 128
        ),
    )(*operands)
    return pl.pallas_call(
        functools.partial(write_kernel, len(shapes)),
        out_shape=shapes,
        in_specs=[anywhere] * len(shapes),
        out_specs=(anywhere,) * len(shapes),
        scratch_shapes=[pltpu.VMEM(one.shape, one.dtype) for one in shapes]
        + [pltpu.SemaphoreType.DMA((2, len(shapes)))],
        compiler_params=pltpu.CompilerParams(vmem_limit_bytes=62 * 1024 * 1024),
    )(*results)


def choose_body(mesh, *arrays):
    rows, width = arrays[0].shape
    seq_count = mesh.shape["seq"]
    fits = width == 64 * seq_count and rows == 128 and seq_count == 16
    if fits and mesh.shape["chan"] == 2:
        return fast_body(*arrays)
    return wide_body(*arrays)


def solution(mesh):
    return jax.shard_map(
        functools.partial(choose_body, mesh),
        mesh=mesh,
        in_specs=(
            P("seq", "chan"),
            P("seq", "chan"),
            P("seq", "chan"),
            P("seq", "chan"),
            P("chan"),
            P("chan"),
            P("seq", "chan"),
        ),
        out_specs=(
            P("seq", "chan"),
            P("seq", "chan"),
            P("seq", "chan"),
            P("seq", "chan"),
            P("seq", "chan"),
        ),
        check_vma=False,
    )
```

```python
import functools
import math

import jax
import jax.numpy as jnp
import numpy as np
from jax import lax
from jax.experimental import pallas as pl
from jax.experimental.pallas import tpu as pltpu
from jax.sharding import PartitionSpec as P

exact_mode = lax.Precision.HIGHEST
epsilon_value = 1e-05


def dft_matrix(count, sign):
    indices = jnp.arange(count, dtype=jnp.int32)
    product = indices[:, None] * indices[None, :] % count
    angles = product.astype(jnp.float32) * (2.0 * math.pi / count)
    cosine = jnp.cos(angles)
    sine_part = sign * jnp.sin(angles)
    return jnp.stack([jnp.stack([cosine, -sine_part], 1), jnp.stack([sine_part, cosine], 1)], 0)


def rotate(field, angles):
    cos_part = jnp.cos(angles)
    sin_part = jnp.sin(angles)
    real_part = field[:, 0]
    imag_part = field[:, 1]
    return jnp.stack(
        [real_part * cos_part - imag_part * sin_part, real_part * sin_part + imag_part * cos_part],
        1,
    )


def prepare(signals, positions, length):
    angles = (positions.astype(jnp.float32) * (-math.pi / length))[..., None]
    cos_part = jnp.cos(angles)
    sin_part = jnp.sin(angles)
    real_in = signals[:, 0]
    real_part = jnp.stack([real_in, real_in * cos_part], 1)
    imag_part = jnp.stack([jnp.zeros_like(real_in), real_in * sin_part], 1)
    return jnp.stack([real_part, imag_part], 1)


def finish(field, positions, length):
    angles = (positions.astype(jnp.float32) * (math.pi / length))[..., None]
    second = rotate(field[:, :, 1], angles)
    return (field[:, :, 0] + second) / (2.0 * length)


def complex_product(first, second, conjugate):
    second_imag = -second[1] if conjugate else second[1]
    return jnp.stack(
        [
            first[0] * second[0] - first[1] * second_imag,
            first[0] * second_imag + first[1] * second[0],
        ],
        0,
    )


def wide_body(query_proj, key_proj, value_proj, long_filter, skip_gain, norm_gain, out_grad):
    tok_rows, chan_width = query_proj.shape
    seq_count = lax.axis_size("seq")
    seq_index = lax.axis_index("seq")
    length = tok_rows * seq_count
    channel_total = chan_width * lax.axis_size("chan")
    narrow_rows = tok_rows // seq_count
    forward_rows = dft_matrix(tok_rows, -1.0)
    inverse_rows = dft_matrix(tok_rows, 1.0)

    def block_places():
        offsets = seq_index * narrow_rows + jnp.arange(narrow_rows, dtype=jnp.int32)
        return jnp.arange(seq_count, dtype=jnp.int32)[:, None] * tok_rows + offsets[None, :]

    def channel_forward(signals):
        batch, width = (signals.shape[0], signals.shape[1])
        blocks = signals.reshape(batch, width, seq_count, narrow_rows, chan_width)
        spread = lax.all_to_all(blocks, "seq", split_axis=2, concat_axis=2, tiled=True)
        field = prepare(spread, block_places(), length)
        field = jnp.einsum(
            "pkqn,bqsnjc->bpskjc", dft_matrix(seq_count, -1.0), field, precision=exact_mode
        )
        offsets = seq_index * narrow_rows + jnp.arange(narrow_rows, dtype=jnp.int32)
        turns = jnp.arange(seq_count, dtype=jnp.int32)[:, None] * offsets[None, :] % length
        field = rotate(field, (turns.astype(jnp.float32) * (-2.0 * math.pi / length))[:, :, None])
        field = lax.all_to_all(field, "seq", split_axis=3, concat_axis=3, tiled=True)
        field = field.reshape(batch, 2, 2, tok_rows, chan_width)
        return jnp.einsum("pkqr,bqsrc->bpskc", forward_rows, field, precision=exact_mode)

    def channel_inverse(spectra, parts):
        batch = spectra.shape[0]
        field = jnp.einsum("pkqr,bqsrc->bpskc", inverse_rows, spectra, precision=exact_mode)
        turns = seq_index * jnp.arange(tok_rows, dtype=jnp.int32) % length
        field = rotate(field, (turns.astype(jnp.float32) * (2.0 * math.pi / length))[:, None])
        field = field.reshape(batch, 2, 2, seq_count, narrow_rows, chan_width)
        field = lax.all_to_all(field, "seq", split_axis=3, concat_axis=3, tiled=True)
        field = jnp.einsum(
            "pkqn,bqsnjc->bpskjc", dft_matrix(seq_count, 1.0), field, precision=exact_mode
        )
        result = finish(field, block_places(), length)[:, :parts]
        result = lax.all_to_all(result, "seq", split_axis=2, concat_axis=2, tiled=True)
        return result.reshape(batch, parts, tok_rows, chan_width)

    def transform(signals):
        return channel_forward(signals)

    def untransform(spectra, parts):
        return channel_inverse(spectra, parts)

    queries = query_proj.astype(jnp.float32)
    key_rows = key_proj.astype(jnp.float32)
    values = value_proj.astype(jnp.float32)
    gated_in = key_rows * values
    spectra = transform(jnp.stack([gated_in, long_filter], 0)[:, None])
    gated_spec = spectra[0]
    filter_spec = spectra[1]
    mixed_spec = complex_product(gated_spec, filter_spec, False)
    convolved = untransform(mixed_spec[None], 1)[0, 0]
    mixed = convolved + skip_gain[None, :] * gated_in
    activated = queries * mixed
    squares = lax.psum(jnp.sum(activated * activated, axis=1), "chan")
    inverse_rms = lax.rsqrt(squares / channel_total + epsilon_value)[:, None]
    block_out = (activated * inverse_rms * norm_gain[None, :]).astype(jnp.bfloat16)
    scaled_grad = out_grad.astype(jnp.float32) * norm_gain[None, :]
    cross_sum = lax.psum(jnp.sum(scaled_grad * activated, axis=1), "chan")
    cross_mean = (cross_sum / channel_total)[:, None]
    act_grad = inverse_rms * scaled_grad - activated * inverse_rms**3 * cross_mean
    query_grad = (act_grad * mixed).astype(jnp.bfloat16)
    mix_grad = act_grad * queries
    grad_spec = transform(mix_grad[None, None])[0]
    toward_input = complex_product(grad_spec, filter_spec, True)
    toward_filter = complex_product(grad_spec, gated_spec, True)
    results = untransform(jnp.stack([toward_input, toward_filter], 0), 1)
    input_part = results[0, 0]
    filter_grad = results[1, 0]
    gated_grad = input_part + skip_gain[None, :] * mix_grad
    key_grad = (gated_grad * values).astype(jnp.bfloat16)
    value_grad = (gated_grad * key_rows).astype(jnp.bfloat16)
    return (block_out, query_grad, key_grad, value_grad, filter_grad)


MESH = pl.DeviceIdType.MESH
GATED, FILTER, CONV, MIXGRAD, INPUT, FGRAD = range(6)


def split_matrix(matrix):
    matrix = jnp.asarray(matrix, jnp.float32)
    high = matrix.astype(jnp.bfloat16)
    low = (matrix - high.astype(jnp.float32)).astype(jnp.bfloat16)
    return jnp.concatenate([high, low, high], 1)


def block_matrices(rows):
    freqs = 2 * np.arange(rows) + 1
    places = np.arange(2 * rows)
    angles = np.pi / (2 * rows) * (freqs[:, None] * places[None, :] % (4 * rows))
    forward = np.concatenate([np.cos(angles), -np.sin(angles)], 0)[:, :rows]
    inverse = np.concatenate([np.cos(angles), -np.sin(angles)], 0)[:, :rows].T / rows
    return split_matrix(forward), split_matrix(inverse)


def split_dot(matrix, values):
    high = values.astype(jnp.bfloat16)
    low = (values - high.astype(jnp.float32)).astype(jnp.bfloat16)
    return jnp.dot(
        matrix, jnp.concatenate([high, high, low], 0), preferred_element_type=jnp.float32
    )


def fast_kernel(
    seq_count,
    q_hbm, k_hbm, v_hbm, f_hbm, skip_hbm, norm_hbm, g_hbm, fwd_hbm, inv_hbm,
    out_hbm, qg_hbm, kg_hbm, vg_hbm, fg_hbm,
    out_ref, qg_ref, kg_ref, vg_ref, fg_ref,
    q_ref, k_ref, v_ref, f_ref, skip_ref, norm_ref, g_ref, fwd_ref, inv_ref,
    send, recv, h_spec, h_swap, x_spec, x_swap, m_spec, m_swap, z_spec,
    even_ref, odd_ref, back_ref,
    mixed_ref, mix_ref, stat_send, stat_recv,
    send_sems, recv_sems, stat_sems, load_sems, store_sems,
):
    rows, width = q_ref.shape
    half = rows // 2
    pairs = seq_count // 2
    channel_total = 2 * width
    me = lax.axis_index("seq")
    core = lax.axis_index("chan")
    f32 = jnp.float32

    loads = [
        pltpu.make_async_copy(source, target, load_sems.at[place])
        for place, (source, target) in enumerate([
            (f_hbm, f_ref), (k_hbm, k_ref), (v_hbm, v_ref), (fwd_hbm, fwd_ref),
            (inv_hbm, inv_ref), (q_hbm, q_ref), (g_hbm, g_ref), (skip_hbm, skip_ref),
            (norm_hbm, norm_ref),
        ])
    ]
    for copy in loads:
        copy.start()
    stores = [
        pltpu.make_async_copy(source, target, store_sems.at[place])
        for place, (source, target) in enumerate([
            (out_ref, out_hbm), (qg_ref, qg_hbm), (kg_ref, kg_hbm), (vg_ref, vg_hbm),
            (fg_ref, fg_hbm),
        ])
    ]

    barrier = pltpu.get_barrier_semaphore()

    def greet(step, carry):
        peer = lax.rem(me + step, seq_count)
        pl.semaphore_signal(barrier, inc=1, device_id={"seq": peer}, device_id_type=MESH)
        return carry

    lax.fori_loop(1, seq_count, greet, 0)
    pl.semaphore_signal(barrier, inc=1, device_id={"chan": 1 - core}, device_id_type=MESH)

    def first_lanes(count):
        return lax.broadcasted_iota(jnp.int32, (count, 128), 1) < 64

    def swap(values):
        return pltpu.roll(values, 64, 1)

    def lanes(tile):
        return pl.ds(pl.multiple_of(tile * 128, 128), 128)

    def pack(unit, tile, values):
        top, bottom = values[:half], values[half:]
        left = first_lanes(half)
        send[unit, 2 * tile] = jnp.where(left, top, swap(bottom))
        send[unit, 2 * tile + 1] = jnp.where(left, swap(top), bottom)

    def unpack(unit, tile):
        first, second = recv[unit, 2 * tile], recv[unit, 2 * tile + 1]
        left = first_lanes(half)
        return jnp.concatenate(
            [jnp.where(left, first, swap(second)), jnp.where(left, swap(first), second)], 0
        )

    def remote(unit, src, dst, peer, send_slot, recv_slot):
        return pltpu.make_async_remote_copy(
            src_ref=send.at[unit, src],
            dst_ref=recv.at[unit, dst],
            send_sem=send_sems.at[unit, send_slot],
            recv_sem=recv_sems.at[unit, recv_slot],
            device_id={"seq": peer},
            device_id_type=MESH,
        )

    my_pair, my_side = me // 2, lax.rem(me, 2)

    def pair_at(flips):
        pair, bit = 0, 1
        while bit < pairs:
            mine, flip = lax.rem(my_pair // bit, 2), lax.rem(flips // bit, 2)
            pair = pair + bit * (mine + flip - 2 * mine * flip)
            bit *= 2
        return pair

    odd_plane = lax.rem(my_pair // 2, 2)

    def send_flips(step):
        later, turn = step // 4, lax.rem(step, 4)
        plane = odd_plane + later - 2 * odd_plane * later
        return 4 * (1 - lax.rem(turn, 2)) + 2 * plane + turn // 2

    def receive_flips(step):
        turn = step // 2
        return 4 * (1 - lax.rem(turn, 2)) + 2 * lax.rem(step, 2) + turn // 2

    def for_peers(flips, use):
        pair = pair_at(flips)
        use(2 * pair + 1 - my_side)

        @pl.when(flips > 0)
        def _():
            use(2 * pair + my_side)

        return pair

    def send_tiles(unit, make):
        def one(step, carry):
            flips = send_flips(step)
            if make is not None:
                pair = pair_at(flips)
                pack(unit, pair, make(pair))
            for_peers(flips, lambda peer: remote(unit, peer, me, peer, peer, me).start())

            @pl.when(flips == 0)
            def _():
                recv[unit, me] = send[unit, me]

            return carry

        lax.fori_loop(0, pairs, one, 0)

    def receive_each(unit, use, carry):
        def one(step, carry):
            pair = for_peers(
                receive_flips(step),
                lambda peer: remote(unit, peer, peer, peer, peer, peer).wait_recv(),
            )
            return use(pair, carry)

        return lax.fori_loop(0, pairs, one, carry)

    def sent_all(unit):
        def one(step, carry):
            for_peers(
                send_flips(step),
                lambda peer: remote(unit, peer, me, peer, peer, me).wait_send(),
            )
            return carry

        lax.fori_loop(0, pairs, one, 0)

    def transform(unit, spec, swapped, pair):
        field = split_dot(fwd_ref[...], unpack(unit, pair))
        spec[pair] = field
        swapped[pair] = swap(field)

    def clear_sums():
        def one(pair, carry):
            z_spec[pair] = jnp.zeros((2 * rows, 128), f32)
            return carry

        lax.fori_loop(0, pairs, one, 0)

    def add_before(spec, swapped, new_spec, new_swapped):
        def one(pair, carry):
            left = first_lanes(rows)
            odd_row = lax.rem(lax.broadcasted_iota(jnp.int32, (rows, 128), 0), 2) == 1
            before = lax.rem(pair + pairs - 1, pairs)
            started = jnp.where(pair > 0, 1.0, 0.0)
            real = jnp.where(left, swapped[before, :rows, :] * started, swapped[pair, :rows, :])
            imag = jnp.where(left, swapped[before, rows:, :] * started, swapped[pair, rows:, :])
            turned_real = jnp.where(odd_row, imag, -imag)
            turned_imag = jnp.where(odd_row, -real, real)
            real = spec[pair, :rows, :] + turned_real
            imag = spec[pair, rows:, :] + turned_imag
            new_spec[pair, :rows, :] = real
            new_spec[pair, rows:, :] = imag
            new_swapped[pair, :rows, :] = swap(real)
            new_swapped[pair, rows:, :] = swap(imag)
            return carry

        lax.fori_loop(0, pairs, one, 0)

    def lay_out(spec, swapped):
        def one(pair, carry):
            left = first_lanes(2 * rows)
            nothing = jnp.zeros((2 * rows, 128), f32)
            even_ref[pair] = nothing
            odd_ref[pair] = nothing
            back_ref[pair] = nothing
            here, there = spec[pair], swapped[pair]
            before = lax.rem(pair + pairs - 1, pairs)
            started = jnp.where(pair > 0, 1.0, 0.0)
            even_ref[pairs + pair] = jnp.where(left, here, there)
            odd_ref[pairs + pair] = jnp.where(left, swapped[before] * started, here)
            back_ref[pairs + pair] = jnp.where(left, there, spec[before] * started)
            return carry

        lax.fori_loop(0, pairs, one, 0)

    def add_products(spec, swapped, pair, forward):
        def one(tile, carry):
            first = pl.multiple_of(tile * 8, 8)
            real_rows, imag_rows = pl.ds(first, 8), pl.ds(first + rows, 8)
            xr, xi = spec[pair, real_rows, :], spec[pair, imag_rows, :]
            yr, yi = swapped[pair, real_rows, :], swapped[pair, imag_rows, :]
            for n in range(pairs):
                if forward:
                    place, cross = pairs + n - pair, odd_ref
                else:
                    place, cross = pairs + pair - n, back_ref
                er, ei = even_ref[place, real_rows, :], even_ref[place, imag_rows, :]
                tr, ti = cross[place, real_rows, :], cross[place, imag_rows, :]
                if forward:
                    real = (xr * er - xi * ei) + (yr * tr - yi * ti)
                    imag = (xr * ei + xi * er) + (yr * ti + yi * tr)
                else:
                    real = (xr * er + xi * ei) + (yr * tr + yi * ti)
                    imag = (xi * er - xr * ei) + (yi * tr - yr * ti)
                z_spec[n, real_rows, :] = z_spec[n, real_rows, :] + real
                z_spec[n, imag_rows, :] = z_spec[n, imag_rows, :] + imag
            return carry

        lax.fori_loop(0, rows // 8, one, 0)

    def load(ref, tile, count):
        first = pl.multiple_of(tile * 8, 8)
        real = [ref[k, pl.ds(first, 8), :] for k in range(count)]
        imag = [ref[k, pl.ds(first + rows, 8), :] for k in range(count)]
        return real, imag

    def correlate(spec, swapped):
        def one(tile, carry):
            left = first_lanes(8)
            zero = jnp.zeros((8, 128), f32)
            hr, hi = load(spec, tile, pairs)
            sr, si = load(swapped, tile, pairs)
            xr, xi = load(m_spec, tile, pairs)
            yr, yi = load(m_swap, tile, pairs)
            even = [
                (jnp.where(left, hr[k], sr[k]), jnp.where(left, hi[k], si[k]))
                for k in range(pairs)
            ]
            odd = [
                (
                    jnp.where(left, sr[k], hr[k - 1] if k else zero),
                    jnp.where(left, si[k], hi[k - 1] if k else zero),
                )
                for k in range(pairs)
            ]
            first = pl.multiple_of(tile * 8, 8)
            for n in range(pairs):
                real, imag = zero, zero
                for k in range(pairs - n):
                    er, ei = even[k]
                    tr, ti = odd[k]
                    m = n + k
                    real = real + (xr[m] * er + xi[m] * ei) + (yr[m] * tr + yi[m] * ti)
                    imag = imag + (xi[m] * er - xr[m] * ei) + (yi[m] * tr - yr[m] * ti)
                z_spec[n, pl.ds(first, 8), :] = real
                z_spec[n, pl.ds(first + rows, 8), :] = imag
            return carry

        lax.fori_loop(0, rows // 8, one, 0)

    def invert(pair):
        return split_dot(inv_ref[...], z_spec[pair])

    def pack_filter(tile, carry):
        pack(FILTER, tile, f_ref[:, lanes(tile)])
        return carry

    def make_gated(tile):
        at = lanes(tile)
        return k_ref[:, at].astype(f32) * v_ref[:, at].astype(f32)

    loads[0].wait()
    lax.fori_loop(0, pairs, pack_filter, 0)
    pl.semaphore_wait(barrier, seq_count)
    send_tiles(FILTER, None)
    for copy in loads[1:3]:
        copy.wait()
    send_tiles(GATED, make_gated)
    for copy in loads[3:]:
        copy.wait()
    clear_sums()

    def take_filter(pair, carry):
        transform(FILTER, h_spec, h_swap, pair)
        return carry

    receive_each(FILTER, take_filter, 0)
    add_before(h_spec, h_swap, m_spec, m_swap)
    lay_out(m_spec, m_swap)

    def take_gated(pair, carry):
        transform(GATED, x_spec, x_swap, pair)
        add_products(x_spec, x_swap, pair, True)
        return carry

    receive_each(GATED, take_gated, 0)
    send_tiles(CONV, invert)
    clear_sums()
    add_before(x_spec, x_swap, h_spec, h_swap)
    sent_all(FILTER)
    sent_all(GATED)

    def activate(tile, carry):
        squares, crosses = carry
        at = lanes(tile)
        gated = k_ref[:, at].astype(f32) * v_ref[:, at].astype(f32)
        mixed = unpack(CONV, tile) + skip_ref[:, at] * gated
        mixed_ref[tile] = mixed
        activated = q_ref[:, at].astype(f32) * mixed
        scaled = g_ref[:, at].astype(f32) * norm_ref[:, at]
        return squares + activated * activated, crosses + scaled * activated

    nothing = jnp.zeros((rows, 128), f32)
    squares, crosses = receive_each(CONV, activate, (nothing, nothing))
    left = first_lanes(rows)
    stat_send[...] = jnp.where(
        left,
        jnp.broadcast_to(jnp.sum(squares, axis=1, keepdims=True), (rows, 128)),
        jnp.broadcast_to(jnp.sum(crosses, axis=1, keepdims=True), (rows, 128)),
    )
    stats = pltpu.make_async_remote_copy(
        src_ref=stat_send,
        dst_ref=stat_recv,
        send_sem=stat_sems.at[0],
        recv_sem=stat_sems.at[1],
        device_id={"chan": 1 - core},
        device_id_type=MESH,
    )
    stats.start()
    stats.wait()
    means = (stat_send[...] + stat_recv[...]) / channel_total
    other = swap(means)
    inverse_rms = lax.rsqrt(jnp.where(left, means, other) + epsilon_value)
    cross_mean = jnp.where(left, other, means)
    cubed = inverse_rms * inverse_rms * inverse_rms * cross_mean

    def differentiate(tile):
        at = lanes(tile)
        queries = q_ref[:, at].astype(f32)
        activated = queries * mixed_ref[tile]
        scaled = g_ref[:, at].astype(f32) * norm_ref[:, at]
        mix_grad = (inverse_rms * scaled - activated * cubed) * queries
        mix_ref[tile] = mix_grad
        return mix_grad

    send_tiles(MIXGRAD, differentiate)

    def first_outputs(tile, carry):
        at = lanes(tile)
        mixed = mixed_ref[tile]
        activated = q_ref[:, at].astype(f32) * mixed
        scaled = g_ref[:, at].astype(f32) * norm_ref[:, at]
        out_ref[:, at] = (activated * inverse_rms * norm_ref[:, at]).astype(out_ref.dtype)
        qg_ref[:, at] = ((inverse_rms * scaled - activated * cubed) * mixed).astype(qg_ref.dtype)
        return carry

    lax.fori_loop(0, pairs, first_outputs, 0)
    for copy in stores[:2]:
        copy.start()
    sent_all(CONV)

    def take_grad(pair, carry):
        transform(MIXGRAD, m_spec, m_swap, pair)
        add_products(m_spec, m_swap, pair, False)
        return carry

    receive_each(MIXGRAD, take_grad, 0)
    send_tiles(INPUT, invert)
    correlate(h_spec, h_swap)
    send_tiles(FGRAD, invert)
    sent_all(MIXGRAD)
    def input_outputs(tile, carry):
        at = lanes(tile)
        gated_grad = unpack(INPUT, tile) + skip_ref[:, at] * mix_ref[tile]
        kg_ref[:, at] = (gated_grad * v_ref[:, at].astype(f32)).astype(kg_ref.dtype)
        vg_ref[:, at] = (gated_grad * k_ref[:, at].astype(f32)).astype(vg_ref.dtype)
        return carry

    receive_each(INPUT, input_outputs, 0)
    for copy in stores[2:4]:
        copy.start()
    sent_all(INPUT)

    def filter_outputs(tile, carry):
        fg_ref[:, lanes(tile)] = unpack(FGRAD, tile)
        return carry

    receive_each(FGRAD, filter_outputs, 0)
    stores[4].start()
    sent_all(FGRAD)
    for copy in stores:
        copy.wait()


def write_kernel(count, *refs):
    read, written, held = (refs[count * part:count * part + count] for part in range(3))
    sems = refs[3 * count]
    inward = [
        pltpu.make_async_copy(read[place], held[place], sems.at[0, place])
        for place in range(count)
    ]
    outward = [
        pltpu.make_async_copy(held[place], written[place], sems.at[1, place])
        for place in range(count)
    ]
    for copy in inward:
        copy.start()
    for first, second in zip(inward, outward):
        first.wait()
        second.start()
    for copy in outward:
        copy.wait()


def fast_body(query_proj, key_proj, value_proj, long_filter, skip_gain, norm_gain, out_grad):
    rows, width = query_proj.shape
    seq_count = lax.axis_size("seq")
    pairs = seq_count // 2
    forward, inverse = block_matrices(rows)
    operands = (
        query_proj, key_proj, value_proj, long_filter,
        skip_gain[None, :], norm_gain[None, :], out_grad, forward, inverse,
    )
    anywhere = pl.BlockSpec(memory_space=pltpu.HBM)
    spec = pltpu.VMEM((pairs, 2 * rows, 128), jnp.float32)
    laid = pltpu.VMEM((2 * pairs, 2 * rows, 128), jnp.float32)
    blocks = pltpu.VMEM((6, seq_count, rows // 2, 128), jnp.float32)
    held = pltpu.VMEM((pairs, rows, 128), jnp.float32)
    stat = pltpu.VMEM((rows, 128), jnp.float32)
    narrow = jax.ShapeDtypeStruct((rows, width), jnp.bfloat16)
    shapes = (narrow,) * 4 + (jax.ShapeDtypeStruct((rows, width), jnp.float32),)
    results = pl.pallas_call(
        functools.partial(fast_kernel, seq_count),
        out_shape=shapes,
        in_specs=[anywhere] * len(operands),
        out_specs=(anywhere,) * 5,
        scratch_shapes=[pltpu.VMEM(one.shape, one.dtype) for one in shapes + operands] + [
            blocks, blocks, spec, spec, spec, spec, spec, spec, spec,
            laid, laid, laid,
            held, held, stat, stat,
            pltpu.SemaphoreType.DMA((6, seq_count)),
            pltpu.SemaphoreType.DMA((6, seq_count)),
            pltpu.SemaphoreType.DMA((2,)),
            pltpu.SemaphoreType.DMA((len(operands),)),
            pltpu.SemaphoreType.DMA((len(shapes),)),
        ],
        compiler_params=pltpu.CompilerParams(
            collective_id=0, has_side_effects=True, vmem_limit_bytes=62 * 1024 * 1024
        ),
        cost_estimate=pl.CostEstimate(
            flops=2 * 10**9, bytes_accessed=4 * 10**6, transcendentals=rows * 128
        ),
    )(*operands)
    return pl.pallas_call(
        functools.partial(write_kernel, len(shapes)),
        out_shape=shapes,
        in_specs=[anywhere] * len(shapes),
        out_specs=(anywhere,) * len(shapes),
        scratch_shapes=[pltpu.VMEM(one.shape, one.dtype) for one in shapes]
        + [pltpu.SemaphoreType.DMA((2, len(shapes)))],
        compiler_params=pltpu.CompilerParams(vmem_limit_bytes=62 * 1024 * 1024),
    )(*results)


def choose_body(mesh, *arrays):
    rows, width = arrays[0].shape
    seq_count = mesh.shape["seq"]
    fits = width == 64 * seq_count and rows == 128 and seq_count == 16
    if fits and mesh.shape["chan"] == 2:
        return fast_body(*arrays)
    return wide_body(*arrays)


def solution(mesh):
    return jax.shard_map(
        functools.partial(choose_body, mesh),
        mesh=mesh,
        in_specs=(
            P("seq", "chan"),
            P("seq", "chan"),
            P("seq", "chan"),
            P("seq", "chan"),
            P("chan"),
            P("chan"),
            P("seq", "chan"),
        ),
        out_specs=(
            P("seq", "chan"),
            P("seq", "chan"),
            P("seq", "chan"),
            P("seq", "chan"),
            P("seq", "chan"),
        ),
        check_vma=False,
    )
```

```python
import functools
import math

import jax
import jax.numpy as jnp
import numpy as np
from jax import lax
from jax.experimental import pallas as pl
from jax.experimental.pallas import tpu as pltpu
from jax.sharding import PartitionSpec as P

exact_mode = lax.Precision.HIGHEST
epsilon_value = 1e-05


def dft_matrix(count, sign):
    indices = jnp.arange(count, dtype=jnp.int32)
    product = indices[:, None] * indices[None, :] % count
    angles = product.astype(jnp.float32) * (2.0 * math.pi / count)
    cosine = jnp.cos(angles)
    sine_part = sign * jnp.sin(angles)
    return jnp.stack([jnp.stack([cosine, -sine_part], 1), jnp.stack([sine_part, cosine], 1)], 0)


def rotate(field, angles):
    cos_part = jnp.cos(angles)
    sin_part = jnp.sin(angles)
    real_part = field[:, 0]
    imag_part = field[:, 1]
    return jnp.stack(
        [real_part * cos_part - imag_part * sin_part, real_part * sin_part + imag_part * cos_part],
        1,
    )


def prepare(signals, positions, length):
    angles = (positions.astype(jnp.float32) * (-math.pi / length))[..., None]
    cos_part = jnp.cos(angles)
    sin_part = jnp.sin(angles)
    real_in = signals[:, 0]
    real_part = jnp.stack([real_in, real_in * cos_part], 1)
    imag_part = jnp.stack([jnp.zeros_like(real_in), real_in * sin_part], 1)
    return jnp.stack([real_part, imag_part], 1)


def finish(field, positions, length):
    angles = (positions.astype(jnp.float32) * (math.pi / length))[..., None]
    second = rotate(field[:, :, 1], angles)
    return (field[:, :, 0] + second) / (2.0 * length)


def complex_product(first, second, conjugate):
    second_imag = -second[1] if conjugate else second[1]
    return jnp.stack(
        [
            first[0] * second[0] - first[1] * second_imag,
            first[0] * second_imag + first[1] * second[0],
        ],
        0,
    )


def wide_body(query_proj, key_proj, value_proj, long_filter, skip_gain, norm_gain, out_grad):
    tok_rows, chan_width = query_proj.shape
    seq_count = lax.axis_size("seq")
    seq_index = lax.axis_index("seq")
    length = tok_rows * seq_count
    channel_total = chan_width * lax.axis_size("chan")
    narrow_rows = tok_rows // seq_count
    forward_rows = dft_matrix(tok_rows, -1.0)
    inverse_rows = dft_matrix(tok_rows, 1.0)

    def block_places():
        offsets = seq_index * narrow_rows + jnp.arange(narrow_rows, dtype=jnp.int32)
        return jnp.arange(seq_count, dtype=jnp.int32)[:, None] * tok_rows + offsets[None, :]

    def channel_forward(signals):
        batch, width = (signals.shape[0], signals.shape[1])
        blocks = signals.reshape(batch, width, seq_count, narrow_rows, chan_width)
        spread = lax.all_to_all(blocks, "seq", split_axis=2, concat_axis=2, tiled=True)
        field = prepare(spread, block_places(), length)
        field = jnp.einsum(
            "pkqn,bqsnjc->bpskjc", dft_matrix(seq_count, -1.0), field, precision=exact_mode
        )
        offsets = seq_index * narrow_rows + jnp.arange(narrow_rows, dtype=jnp.int32)
        turns = jnp.arange(seq_count, dtype=jnp.int32)[:, None] * offsets[None, :] % length
        field = rotate(field, (turns.astype(jnp.float32) * (-2.0 * math.pi / length))[:, :, None])
        field = lax.all_to_all(field, "seq", split_axis=3, concat_axis=3, tiled=True)
        field = field.reshape(batch, 2, 2, tok_rows, chan_width)
        return jnp.einsum("pkqr,bqsrc->bpskc", forward_rows, field, precision=exact_mode)

    def channel_inverse(spectra, parts):
        batch = spectra.shape[0]
        field = jnp.einsum("pkqr,bqsrc->bpskc", inverse_rows, spectra, precision=exact_mode)
        turns = seq_index * jnp.arange(tok_rows, dtype=jnp.int32) % length
        field = rotate(field, (turns.astype(jnp.float32) * (2.0 * math.pi / length))[:, None])
        field = field.reshape(batch, 2, 2, seq_count, narrow_rows, chan_width)
        field = lax.all_to_all(field, "seq", split_axis=3, concat_axis=3, tiled=True)
        field = jnp.einsum(
            "pkqn,bqsnjc->bpskjc", dft_matrix(seq_count, 1.0), field, precision=exact_mode
        )
        result = finish(field, block_places(), length)[:, :parts]
        result = lax.all_to_all(result, "seq", split_axis=2, concat_axis=2, tiled=True)
        return result.reshape(batch, parts, tok_rows, chan_width)

    def transform(signals):
        return channel_forward(signals)

    def untransform(spectra, parts):
        return channel_inverse(spectra, parts)

    queries = query_proj.astype(jnp.float32)
    key_rows = key_proj.astype(jnp.float32)
    values = value_proj.astype(jnp.float32)
    gated_in = key_rows * values
    spectra = transform(jnp.stack([gated_in, long_filter], 0)[:, None])
    gated_spec = spectra[0]
    filter_spec = spectra[1]
    mixed_spec = complex_product(gated_spec, filter_spec, False)
    convolved = untransform(mixed_spec[None], 1)[0, 0]
    mixed = convolved + skip_gain[None, :] * gated_in
    activated = queries * mixed
    squares = lax.psum(jnp.sum(activated * activated, axis=1), "chan")
    inverse_rms = lax.rsqrt(squares / channel_total + epsilon_value)[:, None]
    block_out = (activated * inverse_rms * norm_gain[None, :]).astype(jnp.bfloat16)
    scaled_grad = out_grad.astype(jnp.float32) * norm_gain[None, :]
    cross_sum = lax.psum(jnp.sum(scaled_grad * activated, axis=1), "chan")
    cross_mean = (cross_sum / channel_total)[:, None]
    act_grad = inverse_rms * scaled_grad - activated * inverse_rms**3 * cross_mean
    query_grad = (act_grad * mixed).astype(jnp.bfloat16)
    mix_grad = act_grad * queries
    grad_spec = transform(mix_grad[None, None])[0]
    toward_input = complex_product(grad_spec, filter_spec, True)
    toward_filter = complex_product(grad_spec, gated_spec, True)
    results = untransform(jnp.stack([toward_input, toward_filter], 0), 1)
    input_part = results[0, 0]
    filter_grad = results[1, 0]
    gated_grad = input_part + skip_gain[None, :] * mix_grad
    key_grad = (gated_grad * values).astype(jnp.bfloat16)
    value_grad = (gated_grad * key_rows).astype(jnp.bfloat16)
    return (block_out, query_grad, key_grad, value_grad, filter_grad)


MESH = pl.DeviceIdType.MESH
GATED, FILTER, CONV, MIXGRAD, INPUT, FGRAD = range(6)


def split_matrix(matrix):
    matrix = jnp.asarray(matrix, jnp.float32)
    high = matrix.astype(jnp.bfloat16)
    low = (matrix - high.astype(jnp.float32)).astype(jnp.bfloat16)
    return jnp.concatenate([high, low, high], 1)


def block_matrices(rows):
    freqs = 2 * np.arange(rows) + 1
    places = np.arange(2 * rows)
    angles = np.pi / (2 * rows) * (freqs[:, None] * places[None, :] % (4 * rows))
    forward = np.concatenate([np.cos(angles), -np.sin(angles)], 0)[:, :rows]
    inverse = np.concatenate([np.cos(angles), -np.sin(angles)], 0)[:, :rows].T / rows
    return split_matrix(forward), split_matrix(inverse)


def split_dot(matrix, values):
    high = values.astype(jnp.bfloat16)
    low = (values - high.astype(jnp.float32)).astype(jnp.bfloat16)
    return jnp.dot(
        matrix, jnp.concatenate([high, high, low], 0), preferred_element_type=jnp.float32
    )


def fast_kernel(
    seq_count,
    q_hbm, k_hbm, v_hbm, f_hbm, skip_hbm, norm_hbm, g_hbm, fwd_hbm, inv_hbm,
    out_hbm, qg_hbm, kg_hbm, vg_hbm, fg_hbm,
    out_ref, qg_ref, kg_ref, vg_ref, fg_ref,
    q_ref, k_ref, v_ref, f_ref, skip_ref, norm_ref, g_ref, fwd_ref, inv_ref,
    send, recv, h_spec, h_swap, x_spec, x_swap, m_spec, m_swap, z_spec,
    even_ref, odd_ref, back_ref,
    mixed_ref, mix_ref, stat_send, stat_recv,
    send_sems, recv_sems, stat_sems, load_sems, store_sems,
):
    rows, width = q_ref.shape
    half = rows // 2
    pairs = seq_count // 2
    channel_total = 2 * width
    me = lax.axis_index("seq")
    core = lax.axis_index("chan")
    f32 = jnp.float32

    loads = [
        pltpu.make_async_copy(source, target, load_sems.at[place])
        for place, (source, target) in enumerate([
            (f_hbm, f_ref), (k_hbm, k_ref), (v_hbm, v_ref), (fwd_hbm, fwd_ref),
            (inv_hbm, inv_ref), (q_hbm, q_ref), (g_hbm, g_ref), (skip_hbm, skip_ref),
            (norm_hbm, norm_ref),
        ])
    ]
    for copy in loads:
        copy.start()
    stores = [
        pltpu.make_async_copy(source, target, store_sems.at[place])
        for place, (source, target) in enumerate([
            (out_ref, out_hbm), (qg_ref, qg_hbm), (kg_ref, kg_hbm), (vg_ref, vg_hbm),
            (fg_ref, fg_hbm),
        ])
    ]

    barrier = pltpu.get_barrier_semaphore()

    def greet(step, carry):
        peer = lax.rem(me + step, seq_count)
        pl.semaphore_signal(barrier, inc=1, device_id={"seq": peer}, device_id_type=MESH)
        return carry

    lax.fori_loop(1, seq_count, greet, 0)
    pl.semaphore_signal(barrier, inc=1, device_id={"chan": 1 - core}, device_id_type=MESH)

    def first_lanes(count):
        return lax.broadcasted_iota(jnp.int32, (count, 128), 1) < 64

    def swap(values):
        return pltpu.roll(values, 64, 1)

    def lanes(tile):
        return pl.ds(pl.multiple_of(tile * 128, 128), 128)

    def pack(unit, tile, values):
        top, bottom = values[:half], values[half:]
        left = first_lanes(half)
        send[unit, 2 * tile] = jnp.where(left, top, swap(bottom))
        send[unit, 2 * tile + 1] = jnp.where(left, swap(top), bottom)

    def unpack(unit, tile):
        first, second = recv[unit, 2 * tile], recv[unit, 2 * tile + 1]
        left = first_lanes(half)
        return jnp.concatenate(
            [jnp.where(left, first, swap(second)), jnp.where(left, swap(first), second)], 0
        )

    def remote(unit, src, dst, peer, send_slot, recv_slot):
        return pltpu.make_async_remote_copy(
            src_ref=send.at[unit, src],
            dst_ref=recv.at[unit, dst],
            send_sem=send_sems.at[unit, send_slot],
            recv_sem=recv_sems.at[unit, recv_slot],
            device_id={"seq": peer},
            device_id_type=MESH,
        )

    my_pair, my_side = me // 2, lax.rem(me, 2)

    def pair_at(flips):
        pair, bit = 0, 1
        while bit < pairs:
            mine, flip = lax.rem(my_pair // bit, 2), lax.rem(flips // bit, 2)
            pair = pair + bit * (mine + flip - 2 * mine * flip)
            bit *= 2
        return pair

    odd_plane = lax.rem(my_pair // 2, 2)

    def send_flips(step):
        later, turn = step // 4, lax.rem(step, 4)
        plane = odd_plane + later - 2 * odd_plane * later
        return 4 * (1 - lax.rem(turn, 2)) + 2 * plane + turn // 2

    def receive_flips(step):
        turn = step // 2
        return 4 * (1 - lax.rem(turn, 2)) + 2 * lax.rem(step, 2) + turn // 2

    def for_peers(flips, use):
        pair = pair_at(flips)
        use(2 * pair + 1 - my_side)

        @pl.when(flips > 0)
        def _():
            use(2 * pair + my_side)

        return pair

    def send_tiles(unit, make, first=0, last=pairs):
        def one(step, carry):
            flips = send_flips(step)
            if make is not None:
                pair = pair_at(flips)
                pack(unit, pair, make(pair))
            for_peers(flips, lambda peer: remote(unit, peer, me, peer, peer, me).start())

            @pl.when(flips == 0)
            def _():
                recv[unit, me] = send[unit, me]

            return carry

        lax.fori_loop(first, last, one, 0)

    def receive_each(unit, use, carry, first=0, last=pairs):
        def one(step, carry):
            pair = for_peers(
                receive_flips(step),
                lambda peer: remote(unit, peer, peer, peer, peer, peer).wait_recv(),
            )
            return use(pair, carry)

        return lax.fori_loop(first, last, one, carry)

    def sent_all(unit, first=0, last=pairs):
        def one(step, carry):
            for_peers(
                send_flips(step),
                lambda peer: remote(unit, peer, me, peer, peer, me).wait_send(),
            )
            return carry

        lax.fori_loop(first, last, one, 0)

    def transform(unit, spec, swapped, pair):
        field = split_dot(fwd_ref[...], unpack(unit, pair))
        spec[pair] = field
        swapped[pair] = swap(field)

    def clear_sums():
        def one(pair, carry):
            z_spec[pair] = jnp.zeros((2 * rows, 128), f32)
            return carry

        lax.fori_loop(0, pairs, one, 0)

    def add_before(spec, swapped, new_spec, new_swapped):
        def one(pair, carry):
            left = first_lanes(rows)
            odd_row = lax.rem(lax.broadcasted_iota(jnp.int32, (rows, 128), 0), 2) == 1
            before = lax.rem(pair + pairs - 1, pairs)
            started = jnp.where(pair > 0, 1.0, 0.0)
            real = jnp.where(left, swapped[before, :rows, :] * started, swapped[pair, :rows, :])
            imag = jnp.where(left, swapped[before, rows:, :] * started, swapped[pair, rows:, :])
            turned_real = jnp.where(odd_row, imag, -imag)
            turned_imag = jnp.where(odd_row, -real, real)
            real = spec[pair, :rows, :] + turned_real
            imag = spec[pair, rows:, :] + turned_imag
            new_spec[pair, :rows, :] = real
            new_spec[pair, rows:, :] = imag
            new_swapped[pair, :rows, :] = swap(real)
            new_swapped[pair, rows:, :] = swap(imag)
            return carry

        lax.fori_loop(0, pairs, one, 0)

    def lay_out(spec, swapped):
        def one(pair, carry):
            left = first_lanes(2 * rows)
            nothing = jnp.zeros((2 * rows, 128), f32)
            even_ref[pair] = nothing
            odd_ref[pair] = nothing
            back_ref[pair] = nothing
            here, there = spec[pair], swapped[pair]
            before = lax.rem(pair + pairs - 1, pairs)
            started = jnp.where(pair > 0, 1.0, 0.0)
            even_ref[pairs + pair] = jnp.where(left, here, there)
            odd_ref[pairs + pair] = jnp.where(left, swapped[before] * started, here)
            back_ref[pairs + pair] = jnp.where(left, there, spec[before] * started)
            return carry

        lax.fori_loop(0, pairs, one, 0)

    def add_products(spec, swapped, pair, forward):
        def one(tile, carry):
            first = pl.multiple_of(tile * 8, 8)
            real_rows, imag_rows = pl.ds(first, 8), pl.ds(first + rows, 8)
            xr, xi = spec[pair, real_rows, :], spec[pair, imag_rows, :]
            yr, yi = swapped[pair, real_rows, :], swapped[pair, imag_rows, :]
            for n in range(pairs):
                if forward:
                    place, cross = pairs + n - pair, odd_ref
                else:
                    place, cross = pairs + pair - n, back_ref
                er, ei = even_ref[place, real_rows, :], even_ref[place, imag_rows, :]
                tr, ti = cross[place, real_rows, :], cross[place, imag_rows, :]
                if forward:
                    real = (xr * er - xi * ei) + (yr * tr - yi * ti)
                    imag = (xr * ei + xi * er) + (yr * ti + yi * tr)
                else:
                    real = (xr * er + xi * ei) + (yr * tr + yi * ti)
                    imag = (xi * er - xr * ei) + (yi * tr - yr * ti)
                z_spec[n, real_rows, :] = z_spec[n, real_rows, :] + real
                z_spec[n, imag_rows, :] = z_spec[n, imag_rows, :] + imag
            return carry

        lax.fori_loop(0, rows // 8, one, 0)

    def load(ref, tile, count):
        first = pl.multiple_of(tile * 8, 8)
        real = [ref[k, pl.ds(first, 8), :] for k in range(count)]
        imag = [ref[k, pl.ds(first + rows, 8), :] for k in range(count)]
        return real, imag

    def correlate(spec, swapped):
        def one(tile, carry):
            left = first_lanes(8)
            zero = jnp.zeros((8, 128), f32)
            hr, hi = load(spec, tile, pairs)
            sr, si = load(swapped, tile, pairs)
            xr, xi = load(m_spec, tile, pairs)
            yr, yi = load(m_swap, tile, pairs)
            even = [
                (jnp.where(left, hr[k], sr[k]), jnp.where(left, hi[k], si[k]))
                for k in range(pairs)
            ]
            odd = [
                (
                    jnp.where(left, sr[k], hr[k - 1] if k else zero),
                    jnp.where(left, si[k], hi[k - 1] if k else zero),
                )
                for k in range(pairs)
            ]
            first = pl.multiple_of(tile * 8, 8)
            for n in range(pairs):
                real, imag = zero, zero
                for k in range(pairs - n):
                    er, ei = even[k]
                    tr, ti = odd[k]
                    m = n + k
                    real = real + (xr[m] * er + xi[m] * ei) + (yr[m] * tr + yi[m] * ti)
                    imag = imag + (xi[m] * er - xr[m] * ei) + (yi[m] * tr - yr[m] * ti)
                z_spec[n, pl.ds(first, 8), :] = real
                z_spec[n, pl.ds(first + rows, 8), :] = imag
            return carry

        lax.fori_loop(0, rows // 8, one, 0)

    def invert(pair):
        return split_dot(inv_ref[...], z_spec[pair])

    def pack_filter(tile, carry):
        pack(FILTER, tile, f_ref[:, lanes(tile)])
        return carry

    def make_gated(tile):
        at = lanes(tile)
        return k_ref[:, at].astype(f32) * v_ref[:, at].astype(f32)

    loads[0].wait()
    lax.fori_loop(0, pairs, pack_filter, 0)
    pl.semaphore_wait(barrier, seq_count)
    send_tiles(FILTER, None)
    for copy in loads[1:3]:
        copy.wait()
    send_tiles(GATED, make_gated, 0, pairs // 2)
    for copy in loads[3:]:
        copy.wait()
    clear_sums()

    def take_filter(pair, carry):
        transform(FILTER, h_spec, h_swap, pair)
        return carry

    receive_each(FILTER, take_filter, 0, 0, pairs // 2)
    send_tiles(GATED, make_gated, pairs // 2)
    receive_each(FILTER, take_filter, 0, pairs // 2)
    add_before(h_spec, h_swap, m_spec, m_swap)
    lay_out(m_spec, m_swap)

    def take_gated(pair, carry):
        transform(GATED, x_spec, x_swap, pair)
        add_products(x_spec, x_swap, pair, True)
        return carry

    receive_each(GATED, take_gated, 0)
    send_tiles(CONV, invert)
    clear_sums()
    add_before(x_spec, x_swap, h_spec, h_swap)
    sent_all(FILTER)
    sent_all(GATED)

    def activate(tile, carry):
        squares, crosses = carry
        at = lanes(tile)
        gated = k_ref[:, at].astype(f32) * v_ref[:, at].astype(f32)
        mixed = unpack(CONV, tile) + skip_ref[:, at] * gated
        mixed_ref[tile] = mixed
        activated = q_ref[:, at].astype(f32) * mixed
        scaled = g_ref[:, at].astype(f32) * norm_ref[:, at]
        return squares + activated * activated, crosses + scaled * activated

    nothing = jnp.zeros((rows, 128), f32)
    squares, crosses = receive_each(CONV, activate, (nothing, nothing))
    left = first_lanes(rows)
    stat_send[...] = jnp.where(
        left,
        jnp.broadcast_to(jnp.sum(squares, axis=1, keepdims=True), (rows, 128)),
        jnp.broadcast_to(jnp.sum(crosses, axis=1, keepdims=True), (rows, 128)),
    )
    stats = pltpu.make_async_remote_copy(
        src_ref=stat_send,
        dst_ref=stat_recv,
        send_sem=stat_sems.at[0],
        recv_sem=stat_sems.at[1],
        device_id={"chan": 1 - core},
        device_id_type=MESH,
    )
    stats.start()
    stats.wait()
    means = (stat_send[...] + stat_recv[...]) / channel_total
    other = swap(means)
    inverse_rms = lax.rsqrt(jnp.where(left, means, other) + epsilon_value)
    cross_mean = jnp.where(left, other, means)
    cubed = inverse_rms * inverse_rms * inverse_rms * cross_mean

    def differentiate(tile):
        at = lanes(tile)
        queries = q_ref[:, at].astype(f32)
        activated = queries * mixed_ref[tile]
        scaled = g_ref[:, at].astype(f32) * norm_ref[:, at]
        mix_grad = (inverse_rms * scaled - activated * cubed) * queries
        mix_ref[tile] = mix_grad
        return mix_grad

    send_tiles(MIXGRAD, differentiate, 0, pairs // 2)

    def first_outputs(tile, carry):
        at = lanes(tile)
        mixed = mixed_ref[tile]
        activated = q_ref[:, at].astype(f32) * mixed
        scaled = g_ref[:, at].astype(f32) * norm_ref[:, at]
        out_ref[:, at] = (activated * inverse_rms * norm_ref[:, at]).astype(out_ref.dtype)
        qg_ref[:, at] = ((inverse_rms * scaled - activated * cubed) * mixed).astype(qg_ref.dtype)
        return carry

    lax.fori_loop(0, pairs, first_outputs, 0)
    for copy in stores[:2]:
        copy.start()
    sent_all(CONV)
    sent_all(MIXGRAD, 0, pairs // 4)
    send_tiles(MIXGRAD, differentiate, pairs // 2)

    def take_grad(pair, carry):
        transform(MIXGRAD, m_spec, m_swap, pair)
        add_products(m_spec, m_swap, pair, False)
        return carry

    receive_each(MIXGRAD, take_grad, 0)
    send_tiles(INPUT, invert)
    correlate(h_spec, h_swap)
    send_tiles(FGRAD, invert)
    sent_all(MIXGRAD, pairs // 4)
    def input_outputs(tile, carry):
        at = lanes(tile)
        gated_grad = unpack(INPUT, tile) + skip_ref[:, at] * mix_ref[tile]
        kg_ref[:, at] = (gated_grad * v_ref[:, at].astype(f32)).astype(kg_ref.dtype)
        vg_ref[:, at] = (gated_grad * k_ref[:, at].astype(f32)).astype(vg_ref.dtype)
        return carry

    receive_each(INPUT, input_outputs, 0)
    for copy in stores[2:4]:
        copy.start()
    sent_all(INPUT)

    def filter_outputs(tile, carry):
        fg_ref[:, lanes(tile)] = unpack(FGRAD, tile)
        return carry

    receive_each(FGRAD, filter_outputs, 0)
    stores[4].start()
    sent_all(FGRAD)
    for copy in stores:
        copy.wait()


def write_kernel(count, *refs):
    read, written, held = (refs[count * part:count * part + count] for part in range(3))
    sems = refs[3 * count]
    inward = [
        pltpu.make_async_copy(read[place], held[place], sems.at[0, place])
        for place in range(count)
    ]
    outward = [
        pltpu.make_async_copy(held[place], written[place], sems.at[1, place])
        for place in range(count)
    ]
    for copy in inward:
        copy.start()
    for first, second in zip(inward, outward):
        first.wait()
        second.start()
    for copy in outward:
        copy.wait()


def fast_body(query_proj, key_proj, value_proj, long_filter, skip_gain, norm_gain, out_grad):
    rows, width = query_proj.shape
    seq_count = lax.axis_size("seq")
    pairs = seq_count // 2
    forward, inverse = block_matrices(rows)
    operands = (
        query_proj, key_proj, value_proj, long_filter,
        skip_gain[None, :], norm_gain[None, :], out_grad, forward, inverse,
    )
    anywhere = pl.BlockSpec(memory_space=pltpu.HBM)
    spec = pltpu.VMEM((pairs, 2 * rows, 128), jnp.float32)
    laid = pltpu.VMEM((2 * pairs, 2 * rows, 128), jnp.float32)
    blocks = pltpu.VMEM((6, seq_count, rows // 2, 128), jnp.float32)
    held = pltpu.VMEM((pairs, rows, 128), jnp.float32)
    stat = pltpu.VMEM((rows, 128), jnp.float32)
    narrow = jax.ShapeDtypeStruct((rows, width), jnp.bfloat16)
    shapes = (narrow,) * 4 + (jax.ShapeDtypeStruct((rows, width), jnp.float32),)
    results = pl.pallas_call(
        functools.partial(fast_kernel, seq_count),
        out_shape=shapes,
        in_specs=[anywhere] * len(operands),
        out_specs=(anywhere,) * 5,
        scratch_shapes=[pltpu.VMEM(one.shape, one.dtype) for one in shapes + operands] + [
            blocks, blocks, spec, spec, spec, spec, spec, spec, spec,
            laid, laid, laid,
            held, held, stat, stat,
            pltpu.SemaphoreType.DMA((6, seq_count)),
            pltpu.SemaphoreType.DMA((6, seq_count)),
            pltpu.SemaphoreType.DMA((2,)),
            pltpu.SemaphoreType.DMA((len(operands),)),
            pltpu.SemaphoreType.DMA((len(shapes),)),
        ],
        compiler_params=pltpu.CompilerParams(
            collective_id=0, has_side_effects=True, vmem_limit_bytes=62 * 1024 * 1024
        ),
        cost_estimate=pl.CostEstimate(
            flops=2 * 10**9, bytes_accessed=4 * 10**6, transcendentals=rows * 128
        ),
    )(*operands)
    return pl.pallas_call(
        functools.partial(write_kernel, len(shapes)),
        out_shape=shapes,
        in_specs=[anywhere] * len(shapes),
        out_specs=(anywhere,) * len(shapes),
        scratch_shapes=[pltpu.VMEM(one.shape, one.dtype) for one in shapes]
        + [pltpu.SemaphoreType.DMA((2, len(shapes)))],
        compiler_params=pltpu.CompilerParams(vmem_limit_bytes=62 * 1024 * 1024),
    )(*results)


def choose_body(mesh, *arrays):
    rows, width = arrays[0].shape
    seq_count = mesh.shape["seq"]
    fits = width == 64 * seq_count and rows == 128 and seq_count == 16
    if fits and mesh.shape["chan"] == 2:
        return fast_body(*arrays)
    return wide_body(*arrays)


def solution(mesh):
    return jax.shard_map(
        functools.partial(choose_body, mesh),
        mesh=mesh,
        in_specs=(
            P("seq", "chan"),
            P("seq", "chan"),
            P("seq", "chan"),
            P("seq", "chan"),
            P("chan"),
            P("chan"),
            P("seq", "chan"),
        ),
        out_specs=(
            P("seq", "chan"),
            P("seq", "chan"),
            P("seq", "chan"),
            P("seq", "chan"),
            P("seq", "chan"),
        ),
        check_vma=False,
    )
```

```python
import functools
import math

import jax
import jax.numpy as jnp
import numpy as np
from jax import lax
from jax.experimental import pallas as pl
from jax.experimental.pallas import tpu as pltpu
from jax.sharding import PartitionSpec as P

exact_mode = lax.Precision.HIGHEST
epsilon_value = 1e-05


def dft_matrix(count, sign):
    indices = jnp.arange(count, dtype=jnp.int32)
    product = indices[:, None] * indices[None, :] % count
    angles = product.astype(jnp.float32) * (2.0 * math.pi / count)
    cosine = jnp.cos(angles)
    sine_part = sign * jnp.sin(angles)
    return jnp.stack([jnp.stack([cosine, -sine_part], 1), jnp.stack([sine_part, cosine], 1)], 0)


def rotate(field, angles):
    cos_part = jnp.cos(angles)
    sin_part = jnp.sin(angles)
    real_part = field[:, 0]
    imag_part = field[:, 1]
    return jnp.stack(
        [real_part * cos_part - imag_part * sin_part, real_part * sin_part + imag_part * cos_part],
        1,
    )


def prepare(signals, positions, length):
    angles = (positions.astype(jnp.float32) * (-math.pi / length))[..., None]
    cos_part = jnp.cos(angles)
    sin_part = jnp.sin(angles)
    real_in = signals[:, 0]
    real_part = jnp.stack([real_in, real_in * cos_part], 1)
    imag_part = jnp.stack([jnp.zeros_like(real_in), real_in * sin_part], 1)
    return jnp.stack([real_part, imag_part], 1)


def finish(field, positions, length):
    angles = (positions.astype(jnp.float32) * (math.pi / length))[..., None]
    second = rotate(field[:, :, 1], angles)
    return (field[:, :, 0] + second) / (2.0 * length)


def complex_product(first, second, conjugate):
    second_imag = -second[1] if conjugate else second[1]
    return jnp.stack(
        [
            first[0] * second[0] - first[1] * second_imag,
            first[0] * second_imag + first[1] * second[0],
        ],
        0,
    )


def wide_body(query_proj, key_proj, value_proj, long_filter, skip_gain, norm_gain, out_grad):
    tok_rows, chan_width = query_proj.shape
    seq_count = lax.axis_size("seq")
    seq_index = lax.axis_index("seq")
    length = tok_rows * seq_count
    channel_total = chan_width * lax.axis_size("chan")
    narrow_rows = tok_rows // seq_count
    forward_rows = dft_matrix(tok_rows, -1.0)
    inverse_rows = dft_matrix(tok_rows, 1.0)

    def block_places():
        offsets = seq_index * narrow_rows + jnp.arange(narrow_rows, dtype=jnp.int32)
        return jnp.arange(seq_count, dtype=jnp.int32)[:, None] * tok_rows + offsets[None, :]

    def channel_forward(signals):
        batch, width = (signals.shape[0], signals.shape[1])
        blocks = signals.reshape(batch, width, seq_count, narrow_rows, chan_width)
        spread = lax.all_to_all(blocks, "seq", split_axis=2, concat_axis=2, tiled=True)
        field = prepare(spread, block_places(), length)
        field = jnp.einsum(
            "pkqn,bqsnjc->bpskjc", dft_matrix(seq_count, -1.0), field, precision=exact_mode
        )
        offsets = seq_index * narrow_rows + jnp.arange(narrow_rows, dtype=jnp.int32)
        turns = jnp.arange(seq_count, dtype=jnp.int32)[:, None] * offsets[None, :] % length
        field = rotate(field, (turns.astype(jnp.float32) * (-2.0 * math.pi / length))[:, :, None])
        field = lax.all_to_all(field, "seq", split_axis=3, concat_axis=3, tiled=True)
        field = field.reshape(batch, 2, 2, tok_rows, chan_width)
        return jnp.einsum("pkqr,bqsrc->bpskc", forward_rows, field, precision=exact_mode)

    def channel_inverse(spectra, parts):
        batch = spectra.shape[0]
        field = jnp.einsum("pkqr,bqsrc->bpskc", inverse_rows, spectra, precision=exact_mode)
        turns = seq_index * jnp.arange(tok_rows, dtype=jnp.int32) % length
        field = rotate(field, (turns.astype(jnp.float32) * (2.0 * math.pi / length))[:, None])
        field = field.reshape(batch, 2, 2, seq_count, narrow_rows, chan_width)
        field = lax.all_to_all(field, "seq", split_axis=3, concat_axis=3, tiled=True)
        field = jnp.einsum(
            "pkqn,bqsnjc->bpskjc", dft_matrix(seq_count, 1.0), field, precision=exact_mode
        )
        result = finish(field, block_places(), length)[:, :parts]
        result = lax.all_to_all(result, "seq", split_axis=2, concat_axis=2, tiled=True)
        return result.reshape(batch, parts, tok_rows, chan_width)

    def transform(signals):
        return channel_forward(signals)

    def untransform(spectra, parts):
        return channel_inverse(spectra, parts)

    queries = query_proj.astype(jnp.float32)
    key_rows = key_proj.astype(jnp.float32)
    values = value_proj.astype(jnp.float32)
    gated_in = key_rows * values
    spectra = transform(jnp.stack([gated_in, long_filter], 0)[:, None])
    gated_spec = spectra[0]
    filter_spec = spectra[1]
    mixed_spec = complex_product(gated_spec, filter_spec, False)
    convolved = untransform(mixed_spec[None], 1)[0, 0]
    mixed = convolved + skip_gain[None, :] * gated_in
    activated = queries * mixed
    squares = lax.psum(jnp.sum(activated * activated, axis=1), "chan")
    inverse_rms = lax.rsqrt(squares / channel_total + epsilon_value)[:, None]
    block_out = (activated * inverse_rms * norm_gain[None, :]).astype(jnp.bfloat16)
    scaled_grad = out_grad.astype(jnp.float32) * norm_gain[None, :]
    cross_sum = lax.psum(jnp.sum(scaled_grad * activated, axis=1), "chan")
    cross_mean = (cross_sum / channel_total)[:, None]
    act_grad = inverse_rms * scaled_grad - activated * inverse_rms**3 * cross_mean
    query_grad = (act_grad * mixed).astype(jnp.bfloat16)
    mix_grad = act_grad * queries
    grad_spec = transform(mix_grad[None, None])[0]
    toward_input = complex_product(grad_spec, filter_spec, True)
    toward_filter = complex_product(grad_spec, gated_spec, True)
    results = untransform(jnp.stack([toward_input, toward_filter], 0), 1)
    input_part = results[0, 0]
    filter_grad = results[1, 0]
    gated_grad = input_part + skip_gain[None, :] * mix_grad
    key_grad = (gated_grad * values).astype(jnp.bfloat16)
    value_grad = (gated_grad * key_rows).astype(jnp.bfloat16)
    return (block_out, query_grad, key_grad, value_grad, filter_grad)


MESH = pl.DeviceIdType.MESH
GATED, FILTER, CONV, MIXGRAD, INPUT, FGRAD = range(6)


def split_matrix(matrix):
    matrix = jnp.asarray(matrix, jnp.float32)
    high = matrix.astype(jnp.bfloat16)
    low = (matrix - high.astype(jnp.float32)).astype(jnp.bfloat16)
    return jnp.concatenate([high, low, high], 1)


def block_matrices(rows):
    freqs = 2 * np.arange(rows) + 1
    places = np.arange(2 * rows)
    angles = np.pi / (2 * rows) * (freqs[:, None] * places[None, :] % (4 * rows))
    forward = np.concatenate([np.cos(angles), -np.sin(angles)], 0)[:, :rows]
    inverse = np.concatenate([np.cos(angles), -np.sin(angles)], 0)[:, :rows].T / rows
    return split_matrix(forward), split_matrix(inverse)


def split_dot(matrix, values):
    high = values.astype(jnp.bfloat16)
    low = (values - high.astype(jnp.float32)).astype(jnp.bfloat16)
    return jnp.dot(
        matrix, jnp.concatenate([high, high, low], 0), preferred_element_type=jnp.float32
    )


def fast_kernel(
    seq_count,
    q_hbm, k_hbm, v_hbm, f_hbm, skip_hbm, norm_hbm, g_hbm, fwd_hbm, inv_hbm,
    out_hbm, qg_hbm, kg_hbm, vg_hbm, fg_hbm,
    out_ref, qg_ref, kg_ref, vg_ref, fg_ref,
    q_ref, k_ref, v_ref, f_ref, skip_ref, norm_ref, g_ref, fwd_ref, inv_ref,
    send, recv, h_spec, h_swap, x_spec, x_swap, m_spec, m_swap, z_spec,
    even_ref, odd_ref, back_ref,
    mixed_ref, mix_ref, stat_send, stat_recv,
    send_sems, recv_sems, stat_sems, load_sems, store_sems,
):
    rows, width = q_ref.shape
    half = rows // 2
    pairs = seq_count // 2
    channel_total = 2 * width
    me = lax.axis_index("seq")
    core = lax.axis_index("chan")
    f32 = jnp.float32

    loads = [
        pltpu.make_async_copy(source, target, load_sems.at[place])
        for place, (source, target) in enumerate([
            (f_hbm, f_ref), (k_hbm, k_ref), (v_hbm, v_ref), (fwd_hbm, fwd_ref),
            (inv_hbm, inv_ref), (q_hbm, q_ref), (g_hbm, g_ref), (skip_hbm, skip_ref),
            (norm_hbm, norm_ref),
        ])
    ]
    for copy in loads:
        copy.start()
    stores = [
        pltpu.make_async_copy(source, target, store_sems.at[place])
        for place, (source, target) in enumerate([
            (out_ref, out_hbm), (qg_ref, qg_hbm), (kg_ref, kg_hbm), (vg_ref, vg_hbm),
            (fg_ref, fg_hbm),
        ])
    ]

    barrier = pltpu.get_barrier_semaphore()

    def greet(step, carry):
        peer = lax.rem(me + step, seq_count)
        pl.semaphore_signal(barrier, inc=1, device_id={"seq": peer}, device_id_type=MESH)
        return carry

    lax.fori_loop(1, seq_count, greet, 0)
    pl.semaphore_signal(barrier, inc=1, device_id={"chan": 1 - core}, device_id_type=MESH)

    def first_lanes(count):
        return lax.broadcasted_iota(jnp.int32, (count, 128), 1) < 64

    def swap(values):
        return pltpu.roll(values, 64, 1)

    def lanes(tile):
        return pl.ds(pl.multiple_of(tile * 128, 128), 128)

    def pack(unit, tile, values):
        top, bottom = values[:half], values[half:]
        left = first_lanes(half)
        send[unit, 2 * tile] = jnp.where(left, top, swap(bottom))
        send[unit, 2 * tile + 1] = jnp.where(left, swap(top), bottom)

    def unpack(unit, tile):
        first, second = recv[unit, 2 * tile], recv[unit, 2 * tile + 1]
        left = first_lanes(half)
        return jnp.concatenate(
            [jnp.where(left, first, swap(second)), jnp.where(left, swap(first), second)], 0
        )

    def remote(unit, src, dst, peer, send_slot, recv_slot):
        return pltpu.make_async_remote_copy(
            src_ref=send.at[unit, src],
            dst_ref=recv.at[unit, dst],
            send_sem=send_sems.at[unit, send_slot],
            recv_sem=recv_sems.at[unit, recv_slot],
            device_id={"seq": peer},
            device_id_type=MESH,
        )

    my_pair, my_side = me // 2, lax.rem(me, 2)

    def pair_at(flips):
        pair, bit = 0, 1
        while bit < pairs:
            mine, flip = lax.rem(my_pair // bit, 2), lax.rem(flips // bit, 2)
            pair = pair + bit * (mine + flip - 2 * mine * flip)
            bit *= 2
        return pair

    odd_plane = lax.rem(my_pair // 2, 2)

    def send_flips(step):
        later, turn = step // 4, lax.rem(step, 4)
        plane = odd_plane + later - 2 * odd_plane * later
        return 4 * (1 - lax.rem(turn, 2)) + 2 * plane + turn // 2

    def receive_flips(step):
        turn = step // 2
        return 4 * (1 - lax.rem(turn, 2)) + 2 * lax.rem(step, 2) + turn // 2

    def for_peers(flips, use):
        pair = pair_at(flips)
        use(2 * pair + 1 - my_side)

        @pl.when(flips > 0)
        def _():
            use(2 * pair + my_side)

        return pair

    def send_tiles(unit, make, first=0, last=pairs):
        def one(step, carry):
            flips = send_flips(step)
            if make is not None:
                pair = pair_at(flips)
                pack(unit, pair, make(pair))
            for_peers(flips, lambda peer: remote(unit, peer, me, peer, peer, me).start())

            @pl.when(flips == 0)
            def _():
                recv[unit, me] = send[unit, me]

            return carry

        lax.fori_loop(first, last, one, 0)

    def receive_each(unit, use, carry, first=0, last=pairs):
        def one(step, carry):
            pair = for_peers(
                receive_flips(step),
                lambda peer: remote(unit, peer, peer, peer, peer, peer).wait_recv(),
            )
            return use(pair, carry)

        return lax.fori_loop(first, last, one, carry)

    def sent_all(unit, first=0, last=pairs):
        def one(step, carry):
            for_peers(
                send_flips(step),
                lambda peer: remote(unit, peer, me, peer, peer, me).wait_send(),
            )
            return carry

        lax.fori_loop(first, last, one, 0)

    def transform(unit, spec, swapped, pair):
        field = split_dot(fwd_ref[...], unpack(unit, pair))
        spec[pair] = field
        swapped[pair] = swap(field)

    def clear_sums():
        def one(pair, carry):
            z_spec[pair] = jnp.zeros((2 * rows, 128), f32)
            return carry

        lax.fori_loop(0, pairs, one, 0)

    def add_before(spec, swapped, new_spec, new_swapped):
        def one(pair, carry):
            left = first_lanes(rows)
            odd_row = lax.rem(lax.broadcasted_iota(jnp.int32, (rows, 128), 0), 2) == 1
            before = lax.rem(pair + pairs - 1, pairs)
            started = jnp.where(pair > 0, 1.0, 0.0)
            real = jnp.where(left, swapped[before, :rows, :] * started, swapped[pair, :rows, :])
            imag = jnp.where(left, swapped[before, rows:, :] * started, swapped[pair, rows:, :])
            turned_real = jnp.where(odd_row, imag, -imag)
            turned_imag = jnp.where(odd_row, -real, real)
            real = spec[pair, :rows, :] + turned_real
            imag = spec[pair, rows:, :] + turned_imag
            new_spec[pair, :rows, :] = real
            new_spec[pair, rows:, :] = imag
            new_swapped[pair, :rows, :] = swap(real)
            new_swapped[pair, rows:, :] = swap(imag)
            return carry

        lax.fori_loop(0, pairs, one, 0)

    def lay_out(spec, swapped):
        def one(pair, carry):
            left = first_lanes(2 * rows)
            here, there = spec[pair], swapped[pair]
            before = lax.rem(pair + pairs - 1, pairs)
            started = jnp.where(pair > 0, 1.0, 0.0)
            even_ref[pair] = jnp.where(left, here, there)
            odd_ref[pair] = jnp.where(left, swapped[before] * started, here)
            back_ref[pair] = jnp.where(left, there, spec[before] * started)
            return carry

        lax.fori_loop(0, pairs, one, 0)

    def add_products(spec, swapped, pair, forward):
        def one(n, carry):
            place = n - pair if forward else pair - n
            cross = odd_ref if forward else back_ref

            def some(group, carry):
                for part in range(4):
                    first = pl.multiple_of(group * 32 + part * 8, 8)
                    real_rows, imag_rows = pl.ds(first, 8), pl.ds(first + rows, 8)
                    xr, xi = spec[pair, real_rows, :], spec[pair, imag_rows, :]
                    yr, yi = swapped[pair, real_rows, :], swapped[pair, imag_rows, :]
                    er, ei = even_ref[place, real_rows, :], even_ref[place, imag_rows, :]
                    tr, ti = cross[place, real_rows, :], cross[place, imag_rows, :]
                    if forward:
                        real = (xr * er - xi * ei) + (yr * tr - yi * ti)
                        imag = (xr * ei + xi * er) + (yr * ti + yi * tr)
                    else:
                        real = (xr * er + xi * ei) + (yr * tr + yi * ti)
                        imag = (xi * er - xr * ei) + (yi * tr - yr * ti)
                    z_spec[n, real_rows, :] = z_spec[n, real_rows, :] + real
                    z_spec[n, imag_rows, :] = z_spec[n, imag_rows, :] + imag
                return carry

            return lax.fori_loop(0, rows // 32, some, carry)

        if forward:
            lax.fori_loop(pair, pairs, one, 0)
        else:
            lax.fori_loop(0, pair + 1, one, 0)

    def load(ref, tile, count):
        first = pl.multiple_of(tile * 8, 8)
        real = [ref[k, pl.ds(first, 8), :] for k in range(count)]
        imag = [ref[k, pl.ds(first + rows, 8), :] for k in range(count)]
        return real, imag

    def correlate(spec, swapped):
        def one(tile, carry):
            left = first_lanes(8)
            zero = jnp.zeros((8, 128), f32)
            hr, hi = load(spec, tile, pairs)
            sr, si = load(swapped, tile, pairs)
            xr, xi = load(m_spec, tile, pairs)
            yr, yi = load(m_swap, tile, pairs)
            even = [
                (jnp.where(left, hr[k], sr[k]), jnp.where(left, hi[k], si[k]))
                for k in range(pairs)
            ]
            odd = [
                (
                    jnp.where(left, sr[k], hr[k - 1] if k else zero),
                    jnp.where(left, si[k], hi[k - 1] if k else zero),
                )
                for k in range(pairs)
            ]
            first = pl.multiple_of(tile * 8, 8)
            for n in range(pairs):
                real, imag = zero, zero
                for k in range(pairs - n):
                    er, ei = even[k]
                    tr, ti = odd[k]
                    m = n + k
                    real = real + (xr[m] * er + xi[m] * ei) + (yr[m] * tr + yi[m] * ti)
                    imag = imag + (xi[m] * er - xr[m] * ei) + (yi[m] * tr - yr[m] * ti)
                z_spec[n, pl.ds(first, 8), :] = real
                z_spec[n, pl.ds(first + rows, 8), :] = imag
            return carry

        lax.fori_loop(0, rows // 8, one, 0)

    def invert(pair):
        return split_dot(inv_ref[...], z_spec[pair])

    def pack_filter(tile, carry):
        pack(FILTER, tile, f_ref[:, lanes(tile)])
        return carry

    def make_gated(tile):
        at = lanes(tile)
        return k_ref[:, at].astype(f32) * v_ref[:, at].astype(f32)

    loads[0].wait()
    lax.fori_loop(0, pairs, pack_filter, 0)
    pl.semaphore_wait(barrier, seq_count)
    send_tiles(FILTER, None)
    for copy in loads[1:3]:
        copy.wait()
    send_tiles(GATED, make_gated, 0, pairs // 2)
    for copy in loads[3:]:
        copy.wait()
    clear_sums()

    def take_filter(pair, carry):
        transform(FILTER, h_spec, h_swap, pair)
        return carry

    receive_each(FILTER, take_filter, 0, 0, pairs // 2)
    send_tiles(GATED, make_gated, pairs // 2)
    receive_each(FILTER, take_filter, 0, pairs // 2)
    add_before(h_spec, h_swap, m_spec, m_swap)
    lay_out(m_spec, m_swap)

    def take_gated(pair, carry):
        transform(GATED, x_spec, x_swap, pair)
        add_products(x_spec, x_swap, pair, True)
        return carry

    receive_each(GATED, take_gated, 0)
    send_tiles(CONV, invert)
    clear_sums()
    add_before(x_spec, x_swap, h_spec, h_swap)
    sent_all(FILTER)
    sent_all(GATED)

    def activate(tile, carry):
        squares, crosses = carry
        at = lanes(tile)
        gated = k_ref[:, at].astype(f32) * v_ref[:, at].astype(f32)
        mixed = unpack(CONV, tile) + skip_ref[:, at] * gated
        mixed_ref[tile] = mixed
        activated = q_ref[:, at].astype(f32) * mixed
        scaled = g_ref[:, at].astype(f32) * norm_ref[:, at]
        return squares + activated * activated, crosses + scaled * activated

    nothing = jnp.zeros((rows, 128), f32)
    squares, crosses = receive_each(CONV, activate, (nothing, nothing))
    left = first_lanes(rows)
    stat_send[...] = jnp.where(
        left,
        jnp.broadcast_to(jnp.sum(squares, axis=1, keepdims=True), (rows, 128)),
        jnp.broadcast_to(jnp.sum(crosses, axis=1, keepdims=True), (rows, 128)),
    )
    stats = pltpu.make_async_remote_copy(
        src_ref=stat_send,
        dst_ref=stat_recv,
        send_sem=stat_sems.at[0],
        recv_sem=stat_sems.at[1],
        device_id={"chan": 1 - core},
        device_id_type=MESH,
    )
    stats.start()
    stats.wait()
    means = (stat_send[...] + stat_recv[...]) / channel_total
    other = swap(means)
    inverse_rms = lax.rsqrt(jnp.where(left, means, other) + epsilon_value)
    cross_mean = jnp.where(left, other, means)
    cubed = inverse_rms * inverse_rms * inverse_rms * cross_mean

    def differentiate(tile):
        at = lanes(tile)
        queries = q_ref[:, at].astype(f32)
        activated = queries * mixed_ref[tile]
        scaled = g_ref[:, at].astype(f32) * norm_ref[:, at]
        mix_grad = (inverse_rms * scaled - activated * cubed) * queries
        mix_ref[tile] = mix_grad
        return mix_grad

    send_tiles(MIXGRAD, differentiate, 0, pairs // 2)

    def first_outputs(tile, carry):
        at = lanes(tile)
        mixed = mixed_ref[tile]
        activated = q_ref[:, at].astype(f32) * mixed
        scaled = g_ref[:, at].astype(f32) * norm_ref[:, at]
        out_ref[:, at] = (activated * inverse_rms * norm_ref[:, at]).astype(out_ref.dtype)
        qg_ref[:, at] = ((inverse_rms * scaled - activated * cubed) * mixed).astype(qg_ref.dtype)
        return carry

    lax.fori_loop(0, pairs, first_outputs, 0)
    for copy in stores[:2]:
        copy.start()
    sent_all(CONV)
    sent_all(MIXGRAD, 0, pairs // 4)
    send_tiles(MIXGRAD, differentiate, pairs // 2)

    def take_grad(pair, carry):
        transform(MIXGRAD, m_spec, m_swap, pair)
        add_products(m_spec, m_swap, pair, False)
        return carry

    receive_each(MIXGRAD, take_grad, 0)
    send_tiles(INPUT, invert)
    correlate(h_spec, h_swap)
    send_tiles(FGRAD, invert)
    sent_all(MIXGRAD, pairs // 4)
    def input_outputs(tile, carry):
        at = lanes(tile)
        gated_grad = unpack(INPUT, tile) + skip_ref[:, at] * mix_ref[tile]
        kg_ref[:, at] = (gated_grad * v_ref[:, at].astype(f32)).astype(kg_ref.dtype)
        vg_ref[:, at] = (gated_grad * k_ref[:, at].astype(f32)).astype(vg_ref.dtype)
        return carry

    receive_each(INPUT, input_outputs, 0)
    for copy in stores[2:4]:
        copy.start()
    sent_all(INPUT)

    def filter_outputs(tile, carry):
        fg_ref[:, lanes(tile)] = unpack(FGRAD, tile)
        return carry

    receive_each(FGRAD, filter_outputs, 0)
    stores[4].start()
    sent_all(FGRAD)
    for copy in stores:
        copy.wait()


def write_kernel(count, *refs):
    read, written, held = (refs[count * part:count * part + count] for part in range(3))
    sems = refs[3 * count]
    inward = [
        pltpu.make_async_copy(read[place], held[place], sems.at[0, place])
        for place in range(count)
    ]
    outward = [
        pltpu.make_async_copy(held[place], written[place], sems.at[1, place])
        for place in range(count)
    ]
    for copy in inward:
        copy.start()
    for first, second in zip(inward, outward):
        first.wait()
        second.start()
    for copy in outward:
        copy.wait()


def fast_body(query_proj, key_proj, value_proj, long_filter, skip_gain, norm_gain, out_grad):
    rows, width = query_proj.shape
    seq_count = lax.axis_size("seq")
    pairs = seq_count // 2
    forward, inverse = block_matrices(rows)
    operands = (
        query_proj, key_proj, value_proj, long_filter,
        skip_gain[None, :], norm_gain[None, :], out_grad, forward, inverse,
    )
    anywhere = pl.BlockSpec(memory_space=pltpu.HBM)
    spec = pltpu.VMEM((pairs, 2 * rows, 128), jnp.float32)
    blocks = pltpu.VMEM((6, seq_count, rows // 2, 128), jnp.float32)
    held = pltpu.VMEM((pairs, rows, 128), jnp.float32)
    stat = pltpu.VMEM((rows, 128), jnp.float32)
    narrow = jax.ShapeDtypeStruct((rows, width), jnp.bfloat16)
    shapes = (narrow,) * 4 + (jax.ShapeDtypeStruct((rows, width), jnp.float32),)
    results = pl.pallas_call(
        functools.partial(fast_kernel, seq_count),
        out_shape=shapes,
        in_specs=[anywhere] * len(operands),
        out_specs=(anywhere,) * 5,
        scratch_shapes=[pltpu.VMEM(one.shape, one.dtype) for one in shapes + operands] + [
            blocks, blocks, spec, spec, spec, spec, spec, spec, spec,
            spec, spec, spec,
            held, held, stat, stat,
            pltpu.SemaphoreType.DMA((6, seq_count)),
            pltpu.SemaphoreType.DMA((6, seq_count)),
            pltpu.SemaphoreType.DMA((2,)),
            pltpu.SemaphoreType.DMA((len(operands),)),
            pltpu.SemaphoreType.DMA((len(shapes),)),
        ],
        compiler_params=pltpu.CompilerParams(
            collective_id=0, has_side_effects=True, vmem_limit_bytes=62 * 1024 * 1024
        ),
        cost_estimate=pl.CostEstimate(
            flops=2 * 10**9, bytes_accessed=4 * 10**6, transcendentals=rows * 128
        ),
    )(*operands)
    return pl.pallas_call(
        functools.partial(write_kernel, len(shapes)),
        out_shape=shapes,
        in_specs=[anywhere] * len(shapes),
        out_specs=(anywhere,) * len(shapes),
        scratch_shapes=[pltpu.VMEM(one.shape, one.dtype) for one in shapes]
        + [pltpu.SemaphoreType.DMA((2, len(shapes)))],
        compiler_params=pltpu.CompilerParams(vmem_limit_bytes=62 * 1024 * 1024),
    )(*results)


def choose_body(mesh, *arrays):
    rows, width = arrays[0].shape
    seq_count = mesh.shape["seq"]
    fits = width == 64 * seq_count and rows == 128 and seq_count == 16
    if fits and mesh.shape["chan"] == 2:
        return fast_body(*arrays)
    return wide_body(*arrays)


def solution(mesh):
    return jax.shard_map(
        functools.partial(choose_body, mesh),
        mesh=mesh,
        in_specs=(
            P("seq", "chan"),
            P("seq", "chan"),
            P("seq", "chan"),
            P("seq", "chan"),
            P("chan"),
            P("chan"),
            P("seq", "chan"),
        ),
        out_specs=(
            P("seq", "chan"),
            P("seq", "chan"),
            P("seq", "chan"),
            P("seq", "chan"),
            P("seq", "chan"),
        ),
        check_vma=False,
    )
```

```python
import functools
import math

import jax
import jax.numpy as jnp
import numpy as np
from jax import lax
from jax.experimental import pallas as pl
from jax.experimental.pallas import tpu as pltpu
from jax.sharding import PartitionSpec as P

exact_mode = lax.Precision.HIGHEST
epsilon_value = 1e-05


def dft_matrix(count, sign):
    indices = jnp.arange(count, dtype=jnp.int32)
    product = indices[:, None] * indices[None, :] % count
    angles = product.astype(jnp.float32) * (2.0 * math.pi / count)
    cosine = jnp.cos(angles)
    sine_part = sign * jnp.sin(angles)
    return jnp.stack([jnp.stack([cosine, -sine_part], 1), jnp.stack([sine_part, cosine], 1)], 0)


def rotate(field, angles):
    cos_part = jnp.cos(angles)
    sin_part = jnp.sin(angles)
    real_part = field[:, 0]
    imag_part = field[:, 1]
    return jnp.stack(
        [real_part * cos_part - imag_part * sin_part, real_part * sin_part + imag_part * cos_part],
        1,
    )


def prepare(signals, positions, length):
    angles = (positions.astype(jnp.float32) * (-math.pi / length))[..., None]
    cos_part = jnp.cos(angles)
    sin_part = jnp.sin(angles)
    real_in = signals[:, 0]
    real_part = jnp.stack([real_in, real_in * cos_part], 1)
    imag_part = jnp.stack([jnp.zeros_like(real_in), real_in * sin_part], 1)
    return jnp.stack([real_part, imag_part], 1)


def finish(field, positions, length):
    angles = (positions.astype(jnp.float32) * (math.pi / length))[..., None]
    second = rotate(field[:, :, 1], angles)
    return (field[:, :, 0] + second) / (2.0 * length)


def complex_product(first, second, conjugate):
    second_imag = -second[1] if conjugate else second[1]
    return jnp.stack(
        [
            first[0] * second[0] - first[1] * second_imag,
            first[0] * second_imag + first[1] * second[0],
        ],
        0,
    )


def wide_body(query_proj, key_proj, value_proj, long_filter, skip_gain, norm_gain, out_grad):
    tok_rows, chan_width = query_proj.shape
    seq_count = lax.axis_size("seq")
    seq_index = lax.axis_index("seq")
    length = tok_rows * seq_count
    channel_total = chan_width * lax.axis_size("chan")
    narrow_rows = tok_rows // seq_count
    forward_rows = dft_matrix(tok_rows, -1.0)
    inverse_rows = dft_matrix(tok_rows, 1.0)

    def block_places():
        offsets = seq_index * narrow_rows + jnp.arange(narrow_rows, dtype=jnp.int32)
        return jnp.arange(seq_count, dtype=jnp.int32)[:, None] * tok_rows + offsets[None, :]

    def channel_forward(signals):
        batch, width = (signals.shape[0], signals.shape[1])
        blocks = signals.reshape(batch, width, seq_count, narrow_rows, chan_width)
        spread = lax.all_to_all(blocks, "seq", split_axis=2, concat_axis=2, tiled=True)
        field = prepare(spread, block_places(), length)
        field = jnp.einsum(
            "pkqn,bqsnjc->bpskjc", dft_matrix(seq_count, -1.0), field, precision=exact_mode
        )
        offsets = seq_index * narrow_rows + jnp.arange(narrow_rows, dtype=jnp.int32)
        turns = jnp.arange(seq_count, dtype=jnp.int32)[:, None] * offsets[None, :] % length
        field = rotate(field, (turns.astype(jnp.float32) * (-2.0 * math.pi / length))[:, :, None])
        field = lax.all_to_all(field, "seq", split_axis=3, concat_axis=3, tiled=True)
        field = field.reshape(batch, 2, 2, tok_rows, chan_width)
        return jnp.einsum("pkqr,bqsrc->bpskc", forward_rows, field, precision=exact_mode)

    def channel_inverse(spectra, parts):
        batch = spectra.shape[0]
        field = jnp.einsum("pkqr,bqsrc->bpskc", inverse_rows, spectra, precision=exact_mode)
        turns = seq_index * jnp.arange(tok_rows, dtype=jnp.int32) % length
        field = rotate(field, (turns.astype(jnp.float32) * (2.0 * math.pi / length))[:, None])
        field = field.reshape(batch, 2, 2, seq_count, narrow_rows, chan_width)
        field = lax.all_to_all(field, "seq", split_axis=3, concat_axis=3, tiled=True)
        field = jnp.einsum(
            "pkqn,bqsnjc->bpskjc", dft_matrix(seq_count, 1.0), field, precision=exact_mode
        )
        result = finish(field, block_places(), length)[:, :parts]
        result = lax.all_to_all(result, "seq", split_axis=2, concat_axis=2, tiled=True)
        return result.reshape(batch, parts, tok_rows, chan_width)

    def transform(signals):
        return channel_forward(signals)

    def untransform(spectra, parts):
        return channel_inverse(spectra, parts)

    queries = query_proj.astype(jnp.float32)
    key_rows = key_proj.astype(jnp.float32)
    values = value_proj.astype(jnp.float32)
    gated_in = key_rows * values
    spectra = transform(jnp.stack([gated_in, long_filter], 0)[:, None])
    gated_spec = spectra[0]
    filter_spec = spectra[1]
    mixed_spec = complex_product(gated_spec, filter_spec, False)
    convolved = untransform(mixed_spec[None], 1)[0, 0]
    mixed = convolved + skip_gain[None, :] * gated_in
    activated = queries * mixed
    squares = lax.psum(jnp.sum(activated * activated, axis=1), "chan")
    inverse_rms = lax.rsqrt(squares / channel_total + epsilon_value)[:, None]
    block_out = (activated * inverse_rms * norm_gain[None, :]).astype(jnp.bfloat16)
    scaled_grad = out_grad.astype(jnp.float32) * norm_gain[None, :]
    cross_sum = lax.psum(jnp.sum(scaled_grad * activated, axis=1), "chan")
    cross_mean = (cross_sum / channel_total)[:, None]
    act_grad = inverse_rms * scaled_grad - activated * inverse_rms**3 * cross_mean
    query_grad = (act_grad * mixed).astype(jnp.bfloat16)
    mix_grad = act_grad * queries
    grad_spec = transform(mix_grad[None, None])[0]
    toward_input = complex_product(grad_spec, filter_spec, True)
    toward_filter = complex_product(grad_spec, gated_spec, True)
    results = untransform(jnp.stack([toward_input, toward_filter], 0), 1)
    input_part = results[0, 0]
    filter_grad = results[1, 0]
    gated_grad = input_part + skip_gain[None, :] * mix_grad
    key_grad = (gated_grad * values).astype(jnp.bfloat16)
    value_grad = (gated_grad * key_rows).astype(jnp.bfloat16)
    return (block_out, query_grad, key_grad, value_grad, filter_grad)


MESH = pl.DeviceIdType.MESH
GATED, FILTER, CONV, MIXGRAD, INPUT, FGRAD = range(6)


def split_matrix(matrix):
    matrix = jnp.asarray(matrix, jnp.float32)
    high = matrix.astype(jnp.bfloat16)
    low = (matrix - high.astype(jnp.float32)).astype(jnp.bfloat16)
    return jnp.concatenate([high, low, high], 1)


def block_matrices(rows):
    freqs = 2 * np.arange(rows) + 1
    places = np.arange(2 * rows)
    angles = np.pi / (2 * rows) * (freqs[:, None] * places[None, :] % (4 * rows))
    forward = np.concatenate([np.cos(angles), -np.sin(angles)], 0)[:, :rows]
    inverse = np.concatenate([np.cos(angles), -np.sin(angles)], 0)[:, :rows].T / rows
    return split_matrix(forward), split_matrix(inverse)


def split_dot(matrix, values):
    high = values.astype(jnp.bfloat16)
    low = (values - high.astype(jnp.float32)).astype(jnp.bfloat16)
    return jnp.dot(
        matrix, jnp.concatenate([high, high, low], 0), preferred_element_type=jnp.float32
    )


def fast_kernel(
    seq_count,
    q_hbm, k_hbm, v_hbm, f_hbm, skip_hbm, norm_hbm, g_hbm, fwd_hbm, inv_hbm,
    out_hbm, qg_hbm, kg_hbm, vg_hbm, fg_hbm,
    out_ref, qg_ref, kg_ref, vg_ref, fg_ref,
    q_ref, k_ref, v_ref, f_ref, skip_ref, norm_ref, g_ref, fwd_ref, inv_ref,
    send, recv, h_spec, h_swap, x_spec, x_swap, m_spec, m_swap, z_spec,
    even_ref, odd_ref, back_ref,
    mixed_ref, mix_ref, stat_send, stat_recv,
    send_sems, recv_sems, stat_sems, load_sems, store_sems,
):
    rows, width = q_ref.shape
    half = rows // 2
    pairs = seq_count // 2
    channel_total = 2 * width
    me = lax.axis_index("seq")
    core = lax.axis_index("chan")
    f32 = jnp.float32

    loads = [
        pltpu.make_async_copy(source, target, load_sems.at[place])
        for place, (source, target) in enumerate([
            (f_hbm, f_ref), (k_hbm, k_ref), (v_hbm, v_ref), (fwd_hbm, fwd_ref),
            (inv_hbm, inv_ref), (q_hbm, q_ref), (g_hbm, g_ref), (skip_hbm, skip_ref),
            (norm_hbm, norm_ref),
        ])
    ]
    for copy in loads:
        copy.start()
    stores = [
        pltpu.make_async_copy(source, target, store_sems.at[place])
        for place, (source, target) in enumerate([
            (out_ref, out_hbm), (qg_ref, qg_hbm), (kg_ref, kg_hbm), (vg_ref, vg_hbm),
            (fg_ref, fg_hbm),
        ])
    ]

    barrier = pltpu.get_barrier_semaphore()

    def greet(step, carry):
        peer = lax.rem(me + step, seq_count)
        pl.semaphore_signal(barrier, inc=1, device_id={"seq": peer}, device_id_type=MESH)
        return carry

    lax.fori_loop(1, seq_count, greet, 0)
    pl.semaphore_signal(barrier, inc=1, device_id={"chan": 1 - core}, device_id_type=MESH)

    def first_lanes(count):
        return lax.broadcasted_iota(jnp.int32, (count, 128), 1) < 64

    def swap(values):
        return pltpu.roll(values, 64, 1)

    def lanes(tile):
        return pl.ds(pl.multiple_of(tile * 128, 128), 128)

    def pack(unit, tile, values):
        top, bottom = values[:half], values[half:]
        left = first_lanes(half)
        send[unit, 2 * tile] = jnp.where(left, top, swap(bottom))
        send[unit, 2 * tile + 1] = jnp.where(left, swap(top), bottom)

    def unpack(unit, tile):
        first, second = recv[unit, 2 * tile], recv[unit, 2 * tile + 1]
        left = first_lanes(half)
        return jnp.concatenate(
            [jnp.where(left, first, swap(second)), jnp.where(left, swap(first), second)], 0
        )

    def remote(unit, src, dst, peer, send_slot, recv_slot):
        return pltpu.make_async_remote_copy(
            src_ref=send.at[unit, src],
            dst_ref=recv.at[unit, dst],
            send_sem=send_sems.at[unit, send_slot],
            recv_sem=recv_sems.at[unit, recv_slot],
            device_id={"seq": peer},
            device_id_type=MESH,
        )

    my_pair, my_side = me // 2, lax.rem(me, 2)

    def pair_at(flips):
        pair, bit = 0, 1
        while bit < pairs:
            mine, flip = lax.rem(my_pair // bit, 2), lax.rem(flips // bit, 2)
            pair = pair + bit * (mine + flip - 2 * mine * flip)
            bit *= 2
        return pair

    odd_plane = lax.rem(my_pair // 2, 2)

    def send_flips(step):
        later, turn = step // 4, lax.rem(step, 4)
        plane = odd_plane + later - 2 * odd_plane * later
        return 4 * (1 - lax.rem(turn, 2)) + 2 * plane + turn // 2

    def receive_flips(step):
        turn = step // 2
        return 4 * (1 - lax.rem(turn, 2)) + 2 * lax.rem(step, 2) + turn // 2

    def for_peers(flips, use):
        pair = pair_at(flips)
        use(2 * pair + 1 - my_side)

        @pl.when(flips > 0)
        def _():
            use(2 * pair + my_side)

        return pair

    def send_tiles(unit, make, first=0, last=pairs):
        def one(step, carry):
            flips = send_flips(step)
            if make is not None:
                pair = pair_at(flips)
                pack(unit, pair, make(pair))
            for_peers(flips, lambda peer: remote(unit, peer, me, peer, peer, me).start())

            @pl.when(flips == 0)
            def _():
                recv[unit, me] = send[unit, me]

            return carry

        lax.fori_loop(first, last, one, 0)

    def receive_each(unit, use, carry, first=0, last=pairs):
        def one(step, carry):
            pair = for_peers(
                receive_flips(step),
                lambda peer: remote(unit, peer, peer, peer, peer, peer).wait_recv(),
            )
            return use(pair, carry)

        return lax.fori_loop(first, last, one, carry)

    def sent_all(unit, first=0, last=pairs):
        def one(step, carry):
            for_peers(
                send_flips(step),
                lambda peer: remote(unit, peer, me, peer, peer, me).wait_send(),
            )
            return carry

        lax.fori_loop(first, last, one, 0)

    def transform(unit, spec, swapped, pair):
        field = split_dot(fwd_ref[...], unpack(unit, pair))
        spec[pair] = field
        swapped[pair] = swap(field)

    def clear_sums():
        def one(pair, carry):
            z_spec[pair] = jnp.zeros((2 * rows, 128), f32)
            return carry

        lax.fori_loop(0, pairs, one, 0)

    def add_before(spec, swapped, new_spec, new_swapped):
        def one(pair, carry):
            left = first_lanes(rows)
            odd_row = lax.rem(lax.broadcasted_iota(jnp.int32, (rows, 128), 0), 2) == 1
            before = lax.rem(pair + pairs - 1, pairs)
            started = jnp.where(pair > 0, 1.0, 0.0)
            real = jnp.where(left, swapped[before, :rows, :] * started, swapped[pair, :rows, :])
            imag = jnp.where(left, swapped[before, rows:, :] * started, swapped[pair, rows:, :])
            turned_real = jnp.where(odd_row, imag, -imag)
            turned_imag = jnp.where(odd_row, -real, real)
            real = spec[pair, :rows, :] + turned_real
            imag = spec[pair, rows:, :] + turned_imag
            new_spec[pair, :rows, :] = real
            new_spec[pair, rows:, :] = imag
            new_swapped[pair, :rows, :] = swap(real)
            new_swapped[pair, rows:, :] = swap(imag)
            return carry

        lax.fori_loop(0, pairs, one, 0)

    def lay_out(spec, swapped):
        def one(pair, carry):
            left = first_lanes(2 * rows)
            here, there = spec[pair], swapped[pair]
            before = lax.rem(pair + pairs - 1, pairs)
            started = jnp.where(pair > 0, 1.0, 0.0)
            even_ref[pair] = jnp.where(left, here, there)
            odd_ref[pair] = jnp.where(left, swapped[before] * started, here)
            back_ref[pair] = jnp.where(left, there, spec[before] * started)
            return carry

        lax.fori_loop(0, pairs, one, 0)

    def add_products(spec, swapped, pair, forward):
        cross = odd_ref if forward else back_ref

        def some(group, carry):
            places = []
            for part in range(8):
                first = pl.multiple_of(group * 64 + part * 8, 8)
                places.append((pl.ds(first, 8), pl.ds(first + rows, 8)))
            held = [
                (
                    spec[pair, real_rows, :], spec[pair, imag_rows, :],
                    swapped[pair, real_rows, :], swapped[pair, imag_rows, :],
                )
                for real_rows, imag_rows in places
            ]

            def one(n, carry):
                place = n - pair if forward else pair - n
                for (real_rows, imag_rows), (xr, xi, yr, yi) in zip(places, held):
                    er, ei = even_ref[place, real_rows, :], even_ref[place, imag_rows, :]
                    tr, ti = cross[place, real_rows, :], cross[place, imag_rows, :]
                    if forward:
                        real = (xr * er - xi * ei) + (yr * tr - yi * ti)
                        imag = (xr * ei + xi * er) + (yr * ti + yi * tr)
                    else:
                        real = (xr * er + xi * ei) + (yr * tr + yi * ti)
                        imag = (xi * er - xr * ei) + (yi * tr - yr * ti)
                    z_spec[n, real_rows, :] = z_spec[n, real_rows, :] + real
                    z_spec[n, imag_rows, :] = z_spec[n, imag_rows, :] + imag
                return carry

            if forward:
                return lax.fori_loop(pair, pairs, one, carry)
            return lax.fori_loop(0, pair + 1, one, carry)

        lax.fori_loop(0, rows // 64, some, 0)

    def load(ref, tile, count):
        first = pl.multiple_of(tile * 8, 8)
        real = [ref[k, pl.ds(first, 8), :] for k in range(count)]
        imag = [ref[k, pl.ds(first + rows, 8), :] for k in range(count)]
        return real, imag

    def correlate(spec, swapped):
        def one(tile, carry):
            left = first_lanes(8)
            zero = jnp.zeros((8, 128), f32)
            hr, hi = load(spec, tile, pairs)
            sr, si = load(swapped, tile, pairs)
            xr, xi = load(m_spec, tile, pairs)
            yr, yi = load(m_swap, tile, pairs)
            even = [
                (jnp.where(left, hr[k], sr[k]), jnp.where(left, hi[k], si[k]))
                for k in range(pairs)
            ]
            odd = [
                (
                    jnp.where(left, sr[k], hr[k - 1] if k else zero),
                    jnp.where(left, si[k], hi[k - 1] if k else zero),
                )
                for k in range(pairs)
            ]
            first = pl.multiple_of(tile * 8, 8)
            for n in range(pairs):
                real, imag = zero, zero
                for k in range(pairs - n):
                    er, ei = even[k]
                    tr, ti = odd[k]
                    m = n + k
                    real = real + (xr[m] * er + xi[m] * ei) + (yr[m] * tr + yi[m] * ti)
                    imag = imag + (xi[m] * er - xr[m] * ei) + (yi[m] * tr - yr[m] * ti)
                z_spec[n, pl.ds(first, 8), :] = real
                z_spec[n, pl.ds(first + rows, 8), :] = imag
            return carry

        lax.fori_loop(0, rows // 8, one, 0)

    def invert(pair):
        return split_dot(inv_ref[...], z_spec[pair])

    def pack_filter(tile, carry):
        pack(FILTER, tile, f_ref[:, lanes(tile)])
        return carry

    def make_gated(tile):
        at = lanes(tile)
        return k_ref[:, at].astype(f32) * v_ref[:, at].astype(f32)

    loads[0].wait()
    lax.fori_loop(0, pairs, pack_filter, 0)
    pl.semaphore_wait(barrier, seq_count)
    send_tiles(FILTER, None)
    for copy in loads[1:3]:
        copy.wait()
    send_tiles(GATED, make_gated, 0, pairs // 2)
    for copy in loads[3:]:
        copy.wait()
    clear_sums()

    def take_filter(pair, carry):
        transform(FILTER, h_spec, h_swap, pair)
        return carry

    receive_each(FILTER, take_filter, 0, 0, pairs // 2)
    send_tiles(GATED, make_gated, pairs // 2)
    receive_each(FILTER, take_filter, 0, pairs // 2)
    add_before(h_spec, h_swap, m_spec, m_swap)
    lay_out(m_spec, m_swap)

    def take_gated(pair, carry):
        transform(GATED, x_spec, x_swap, pair)
        add_products(x_spec, x_swap, pair, True)
        return carry

    receive_each(GATED, take_gated, 0)
    send_tiles(CONV, invert)
    clear_sums()
    add_before(x_spec, x_swap, h_spec, h_swap)
    sent_all(FILTER)
    sent_all(GATED)

    def activate(tile, carry):
        squares, crosses = carry
        at = lanes(tile)
        gated = k_ref[:, at].astype(f32) * v_ref[:, at].astype(f32)
        mixed = unpack(CONV, tile) + skip_ref[:, at] * gated
        mixed_ref[tile] = mixed
        activated = q_ref[:, at].astype(f32) * mixed
        scaled = g_ref[:, at].astype(f32) * norm_ref[:, at]
        return squares + activated * activated, crosses + scaled * activated

    nothing = jnp.zeros((rows, 128), f32)
    squares, crosses = receive_each(CONV, activate, (nothing, nothing))
    left = first_lanes(rows)
    stat_send[...] = jnp.where(
        left,
        jnp.broadcast_to(jnp.sum(squares, axis=1, keepdims=True), (rows, 128)),
        jnp.broadcast_to(jnp.sum(crosses, axis=1, keepdims=True), (rows, 128)),
    )
    stats = pltpu.make_async_remote_copy(
        src_ref=stat_send,
        dst_ref=stat_recv,
        send_sem=stat_sems.at[0],
        recv_sem=stat_sems.at[1],
        device_id={"chan": 1 - core},
        device_id_type=MESH,
    )
    stats.start()
    stats.wait()
    means = (stat_send[...] + stat_recv[...]) / channel_total
    other = swap(means)
    inverse_rms = lax.rsqrt(jnp.where(left, means, other) + epsilon_value)
    cross_mean = jnp.where(left, other, means)
    cubed = inverse_rms * inverse_rms * inverse_rms * cross_mean

    def differentiate(tile):
        at = lanes(tile)
        queries = q_ref[:, at].astype(f32)
        activated = queries * mixed_ref[tile]
        scaled = g_ref[:, at].astype(f32) * norm_ref[:, at]
        mix_grad = (inverse_rms * scaled - activated * cubed) * queries
        mix_ref[tile] = mix_grad
        return mix_grad

    send_tiles(MIXGRAD, differentiate, 0, pairs // 2)

    def first_outputs(tile, carry):
        at = lanes(tile)
        mixed = mixed_ref[tile]
        activated = q_ref[:, at].astype(f32) * mixed
        scaled = g_ref[:, at].astype(f32) * norm_ref[:, at]
        out_ref[:, at] = (activated * inverse_rms * norm_ref[:, at]).astype(out_ref.dtype)
        qg_ref[:, at] = ((inverse_rms * scaled - activated * cubed) * mixed).astype(qg_ref.dtype)
        return carry

    lax.fori_loop(0, pairs, first_outputs, 0)
    for copy in stores[:2]:
        copy.start()
    sent_all(CONV)
    sent_all(MIXGRAD, 0, pairs // 4)
    send_tiles(MIXGRAD, differentiate, pairs // 2)

    def take_grad(pair, carry):
        transform(MIXGRAD, m_spec, m_swap, pair)
        add_products(m_spec, m_swap, pair, False)
        return carry

    receive_each(MIXGRAD, take_grad, 0)
    send_tiles(INPUT, invert)
    correlate(h_spec, h_swap)
    send_tiles(FGRAD, invert)
    sent_all(MIXGRAD, pairs // 4)
    def input_outputs(tile, carry):
        at = lanes(tile)
        gated_grad = unpack(INPUT, tile) + skip_ref[:, at] * mix_ref[tile]
        kg_ref[:, at] = (gated_grad * v_ref[:, at].astype(f32)).astype(kg_ref.dtype)
        vg_ref[:, at] = (gated_grad * k_ref[:, at].astype(f32)).astype(vg_ref.dtype)
        return carry

    receive_each(INPUT, input_outputs, 0)
    for copy in stores[2:4]:
        copy.start()
    sent_all(INPUT)

    def filter_outputs(tile, carry):
        fg_ref[:, lanes(tile)] = unpack(FGRAD, tile)
        return carry

    receive_each(FGRAD, filter_outputs, 0)
    stores[4].start()
    sent_all(FGRAD)
    for copy in stores:
        copy.wait()


def write_kernel(count, *refs):
    read, written, held = (refs[count * part:count * part + count] for part in range(3))
    sems = refs[3 * count]
    inward = [
        pltpu.make_async_copy(read[place], held[place], sems.at[0, place])
        for place in range(count)
    ]
    outward = [
        pltpu.make_async_copy(held[place], written[place], sems.at[1, place])
        for place in range(count)
    ]
    for copy in inward:
        copy.start()
    for first, second in zip(inward, outward):
        first.wait()
        second.start()
    for copy in outward:
        copy.wait()


def fast_body(query_proj, key_proj, value_proj, long_filter, skip_gain, norm_gain, out_grad):
    rows, width = query_proj.shape
    seq_count = lax.axis_size("seq")
    pairs = seq_count // 2
    forward, inverse = block_matrices(rows)
    operands = (
        query_proj, key_proj, value_proj, long_filter,
        skip_gain[None, :], norm_gain[None, :], out_grad, forward, inverse,
    )
    anywhere = pl.BlockSpec(memory_space=pltpu.HBM)
    spec = pltpu.VMEM((pairs, 2 * rows, 128), jnp.float32)
    blocks = pltpu.VMEM((6, seq_count, rows // 2, 128), jnp.float32)
    held = pltpu.VMEM((pairs, rows, 128), jnp.float32)
    stat = pltpu.VMEM((rows, 128), jnp.float32)
    narrow = jax.ShapeDtypeStruct((rows, width), jnp.bfloat16)
    shapes = (narrow,) * 4 + (jax.ShapeDtypeStruct((rows, width), jnp.float32),)
    results = pl.pallas_call(
        functools.partial(fast_kernel, seq_count),
        out_shape=shapes,
        in_specs=[anywhere] * len(operands),
        out_specs=(anywhere,) * 5,
        scratch_shapes=[pltpu.VMEM(one.shape, one.dtype) for one in shapes + operands] + [
            blocks, blocks, spec, spec, spec, spec, spec, spec, spec,
            spec, spec, spec,
            held, held, stat, stat,
            pltpu.SemaphoreType.DMA((6, seq_count)),
            pltpu.SemaphoreType.DMA((6, seq_count)),
            pltpu.SemaphoreType.DMA((2,)),
            pltpu.SemaphoreType.DMA((len(operands),)),
            pltpu.SemaphoreType.DMA((len(shapes),)),
        ],
        compiler_params=pltpu.CompilerParams(
            collective_id=0, has_side_effects=True, vmem_limit_bytes=62 * 1024 * 1024
        ),
        cost_estimate=pl.CostEstimate(
            flops=2 * 10**9, bytes_accessed=4 * 10**6, transcendentals=rows * 128
        ),
    )(*operands)
    return pl.pallas_call(
        functools.partial(write_kernel, len(shapes)),
        out_shape=shapes,
        in_specs=[anywhere] * len(shapes),
        out_specs=(anywhere,) * len(shapes),
        scratch_shapes=[pltpu.VMEM(one.shape, one.dtype) for one in shapes]
        + [pltpu.SemaphoreType.DMA((2, len(shapes)))],
        compiler_params=pltpu.CompilerParams(vmem_limit_bytes=62 * 1024 * 1024),
    )(*results)


def choose_body(mesh, *arrays):
    rows, width = arrays[0].shape
    seq_count = mesh.shape["seq"]
    fits = width == 64 * seq_count and rows == 128 and seq_count == 16
    if fits and mesh.shape["chan"] == 2:
        return fast_body(*arrays)
    return wide_body(*arrays)


def solution(mesh):
    return jax.shard_map(
        functools.partial(choose_body, mesh),
        mesh=mesh,
        in_specs=(
            P("seq", "chan"),
            P("seq", "chan"),
            P("seq", "chan"),
            P("seq", "chan"),
            P("chan"),
            P("chan"),
            P("seq", "chan"),
        ),
        out_specs=(
            P("seq", "chan"),
            P("seq", "chan"),
            P("seq", "chan"),
            P("seq", "chan"),
            P("seq", "chan"),
        ),
        check_vma=False,
    )
```
